512 devices in a mesh: pipe: 8 (over y), dp: 64 (over z, x, core).
Axes of the slice: x: 4, y: 8, z: 8, core: 2. Of those that a mesh axis runs over, the one named last changes fastest.
Arguments:
- rollout_rows: bfloat16 [8, 64, 64, 2, 8192], P('pipe', 'dp'), may hold values from -1000 to 1000, as said below
- counts: int32 [8, 64, 64], P('pipe', 'dp'), may hold values from 0 to 2, as said below
- targets: int32 [64, 8, 64], P('dp'), may hold values from 0 to 3071
- final_gain: float32 [8192], replicated, may hold values from 0.5 to 1.5
- lm_head: bfloat16 [8192, 3072], P('dp', 'pipe'), may hold values from -1 to 1
Outputs:
- log_probs: float32 [8, 64, 64], P('pipe', 'dp')
The draws below stay inside these ranges and needn't reach their ends.
Inputs may be any that keep to these rules, and one draw needn't show every extreme that they name: For every micro-batch and learner the counts over owners sum to 64; every learner receives exactly 2 rows from some owner, and some owners send it nothing. `rollout_rows`: slots k >= counts[p, d, o] hold rows that no learner reads.
All inputs are finite; a program needn't handle non-finite values.
Results may differ from the reference program's by a relative error of at most 0.0011.
Values may be sent and summed in bfloat16 or wider, within the bound.
A program may use at most 64 MiB of HBM per device.

```python
import math
import jax
import jax.numpy as jnp
import numpy as np
from jax import lax

D = 8192
MB = 64
VOCAB = 3072
CAP = 2
N_PIPE = 8
N_DP = 64


def count_table(key):
    lower_bound = (MB + N_DP - 1) // N_DP

    def learner_counts(subkey):
        first_key, second_key = jax.random.split(subkey)
        offers = jax.random.randint(first_key, (N_DP,), lower_bound, CAP + 1)
        offers = offers.at[0].set(CAP)
        before = jnp.cumsum(offers) - offers
        taken = jnp.clip(MB - before, 0, offers)
        ordering = jax.random.permutation(second_key, N_DP)
        return taken[ordering]
    subkeys = jax.random.split(key, N_PIPE * N_DP)
    table = jax.vmap(learner_counts)(subkeys)
    return table.reshape(N_PIPE, N_DP, N_DP).astype(jnp.int32)


def head_table(key):
    first_key, second_key = jax.random.split(key, 2)
    spread = jnp.exp(jax.random.uniform(first_key, (VOCAB,), jnp.float32) * math.log(10.0))
    rising = 3.0 ** (jnp.arange(VOCAB, dtype=jnp.float32) / max(VOCAB - 1, 1))
    base = jnp.clip(jax.random.normal(second_key, (D, VOCAB), jnp.float32), -4.0, 4.0)
    table = base * (spread * rising)[None, :] * (0.5 / math.sqrt(D))
    return table


def draw_counts(key, part):
    return count_table(jax.random.fold_in(key, 11))


def draw_lm_head(key, part):
    table = head_table(jax.random.fold_in(key, 23))
    return table.astype(jnp.bfloat16)


def draw_rollout_rows(key, part):
    first_key, second_key, third_key = jax.random.split(jax.random.fold_in(key, 37), 3)
    shape_rows = (N_PIPE, N_DP, N_DP, CAP, D)
    chan_scale = jnp.exp(jax.random.uniform(second_key, (D,), jnp.float32) * math.log(10.0))
    row_scale = jnp.exp(jax.random.uniform(first_key, (N_PIPE, N_DP, N_DP, CAP, 1), jnp.float32) * math.log(10.0))
    noise = jnp.clip(jax.random.normal(third_key, shape_rows, jnp.float32), -6.0, 6.0)
    return (noise * row_scale * chan_scale).astype(jnp.bfloat16)


def touch_ends(values, rng, low, high):
    extent = values.shape
    place = [jax.random.randint(jax.random.fold_in(rng, axis), (), 0, extent[axis]) for axis in range(len(extent))]
    values = values.at[tuple(place)].set(low)
    longest = extent.index(max(extent))
    place[longest] = (place[longest] + 1) % extent[longest]
    return values.at[tuple(place)].set(high)


def rank_bounds(amount, lean):
    loads = [(1 << 20) // math.isqrt(standing ** lean) + 1 for standing in range(1, amount + 1)]
    scale = 1 + sum(loads) // (1 << 30)
    return np.cumsum(np.array([max(1, weight // scale) for weight in loads]))


def ranked(rng, shape, count, skew):
    listing = rank_bounds(count, skew)
    ticket = jax.random.randint(jax.random.fold_in(rng, 1), shape, 0, int(listing[count - 1]))
    rank = jnp.searchsorted(jnp.asarray(listing, jnp.int32), ticket, side="right")
    return jax.random.permutation(jax.random.fold_in(rng, 2), count)[rank].astype(jnp.int32)


def setup_inputs(seed: int = 0) -> dict:
    streams_of = jax.random.split(jax.random.key(seed), 6)
    rollout_rows = draw_rollout_rows(jax.random.fold_in(streams_of[5], 71), 0)
    counts = draw_counts(jax.random.fold_in(streams_of[5], 71), 0)
    targets = touch_ends(ranked(streams_of[2], (N_DP, N_PIPE, MB), VOCAB, 2), jax.random.fold_in(streams_of[2], 3), 0, VOCAB - 1).astype(jnp.int32)
    final_gain = jnp.clip(1.0 + 0.1 * jax.random.normal(streams_of[3], (D,), jnp.float32), 0.5, 1.5)
    lm_head = draw_lm_head(jax.random.fold_in(streams_of[5], 71), 0)
    return {"rollout_rows": rollout_rows, "counts": counts, "targets": targets, "final_gain": final_gain, "lm_head": lm_head}


def reference(rollout_rows, counts, targets, final_gain, lm_head):
    ends_all = jnp.cumsum(counts, axis=-1).astype(jnp.int32)
    starts_all = (ends_all - counts).astype(jnp.int32)
    position = jnp.arange(MB, dtype=jnp.int32)
    owner_index = lax.optimization_barrier(jnp.sum((ends_all[:, :, None, :] <= position[None, None, :, None]).astype(jnp.int32), axis=-1)).astype(jnp.int32)
    offset_row = (position[None, None, :] - jnp.take_along_axis(starts_all, owner_index, axis=-1)).astype(jnp.int32)
    section_index = jnp.arange(N_PIPE, dtype=jnp.int32)[:, None, None]
    learner_index = jnp.arange(N_DP, dtype=jnp.int32)[None, :, None]
    source_index = (((section_index * N_DP + owner_index) * N_DP + learner_index) * CAP + offset_row).astype(jnp.int32)
    flat_rows = rollout_rows.reshape(-1, D)
    section_targets = jnp.transpose(targets, (1, 0, 2)).reshape(N_PIPE, N_DP * MB)

    def one_section(operands):
        index_list, wanted = operands
        gathered = jnp.take(flat_rows, index_list, axis=0).astype(jnp.float32)
        scaling = lax.rsqrt(lax.optimization_barrier(jnp.mean(gathered * gathered, axis=-1, keepdims=True)) + 1e-06)
        normed = (gathered * scaling * final_gain).astype(jnp.bfloat16)
        logits = jnp.dot(normed, lm_head, preferred_element_type=jnp.float32)
        largest = lax.optimization_barrier(jnp.max(logits, axis=-1))
        log_total = jnp.log(lax.optimization_barrier(jnp.sum(jnp.exp(logits - largest[:, None]), axis=-1))) + largest
        picked = jnp.take_along_axis(logits, wanted[:, None], axis=-1)[:, 0]
        return picked - log_total
    result = lax.map(one_section, (source_index.reshape(N_PIPE, N_DP * MB), section_targets))
    return result.reshape(N_PIPE, N_DP, MB)
```

```python
import jax
import jax.numpy as jnp
from jax import lax
from jax.experimental import pallas as pl
from jax.experimental.pallas import tpu as pltpu
from jax.sharding import PartitionSpec as P

NX, NY, NZ, NC = 4, 8, 8, 2
ROWS = 128
FEATURES = 8192
COLS = 384
DEPTH = FEATURES // NZ
PIECE = 128
NQ = 4
QD = DEPTH // NQ
NR = 4
RC = ROWS // NR
MESH = pl.DeviceIdType.MESH


def kernel(x_in, w_in, out_ref, xbuf, wbuf, acc, y_send, y_recv, p_send, p_recv, p_own,
           zp_send, zp_recv, zm_send, zm_recv, xr_send, xr_recv, xl_send, xl_recv,
           s_send, s_recv, own_sem, out_sem):
    y = lax.axis_index("pipe")
    dp = lax.axis_index("dp")
    c = lax.rem(dp, 2)
    x = lax.rem(dp // 2, NX)
    z = dp // (2 * NX)

    def at(zz, xx, cc):
        return (zz * NX + xx) * 2 + cc

    right = (y, at(z, lax.rem(x + 1, NX), c))
    left = (y, at(z, lax.rem(x + NX - 1, NX), c))
    sibling = (y, at(z, x, 1 - c))
    up_z = (y, at(lax.rem(z + 1, NZ), x, c))
    down_z = (y, at(lax.rem(z + NZ - 1, NZ), x, c))
    up_y = (lax.rem(y + 1, NY), dp)
    down_y = (lax.rem(y + NY - 1, NY), dp)
    root_dp = z * 8 + y
    me8 = lax.rem(dp, 8)
    dy = lax.rem(y - me8 + NY, NY)

    barrier = pltpu.get_barrier_semaphore()
    for step in range(1, 8):
        pl.semaphore_signal(barrier, inc=1, device_id=(y, z * 8 + lax.rem(me8 + step, 8)), device_id_type=MESH)
    for other in (up_z, down_z, up_y, down_y):
        pl.semaphore_signal(barrier, inc=1, device_id=other, device_id_type=MESH)
    pl.semaphore_wait(barrier, 11)

    def remote(src, dst, send, recv, device):
        return pltpu.make_async_remote_copy(
            src_ref=src, dst_ref=dst, send_sem=send, recv_sem=recv, device_id=device, device_id_type=MESH)

    def shard_copy():
        return remote(w_in, wbuf.at[0, pl.ds(pl.multiple_of(me8 * PIECE, PIECE), PIECE)],
                      p_send.at[0], p_recv.at[me8], (y, root_dp))

    @pl.when(dy != 0)
    def _():
        shard_copy().start()

    def own_shard():
        return pltpu.make_async_copy(
            w_in, wbuf.at[0, pl.ds(pl.multiple_of(me8 * PIECE, PIECE), PIECE)], p_own.at[0])

    @pl.when(dy == 0)
    def _():
        own_shard().start()

    def rows(ref, i):
        return ref.at[pl.ds(i * RC, RC)]

    def x_right(i):
        return remote(rows(x_in, i), rows(xbuf.at[1, 0], i), xr_send.at[i], xr_recv.at[i], right)

    def x_left(i):
        return remote(rows(x_in, i), rows(xbuf.at[3, 0], i), xl_send.at[i], xl_recv.at[i], left)

    def f_right(i):
        return remote(rows(xbuf.at[1, 0], i), rows(xbuf.at[2, 0], i), xr_send.at[NR + i], xr_recv.at[NR + i], right)

    def sib(d, i):
        src = rows(x_in, i) if d == 0 else rows(xbuf.at[d, 0], i)
        return remote(src, rows(xbuf.at[d, 1], i), s_send.at[d, i], s_recv.at[d, i], sibling)

    own = pltpu.make_async_copy(x_in, xbuf.at[0, 0], own_sem.at[0])
    for i in range(NR):
        x_right(i).start()
        x_left(NR - 1 - i).start()
    own.start()
    for i in range(NR):
        sib(0, i).start()

    def chunk(s, q):
        return wbuf.at[s, pl.ds(q * QD, QD)]

    def y_copy(q, device):
        return remote(chunk(0, q), chunk(0, q), y_send.at[q], y_recv.at[q], device)

    def zp(s, q):
        return remote(chunk(s, q), chunk(s + 1, q), zp_send.at[s, q], zp_recv.at[s, q], up_z)

    def zm(s, q):
        return remote(chunk((8 - s) % 8, q), chunk(7 - s, q), zm_send.at[s, q], zm_recv.at[s, q], down_z)

    def p_wait(i):
        remote(w_in, wbuf.at[0, pl.ds(i * PIECE, PIECE)], p_send.at[0], p_recv.at[i], right).wait_recv()

    def sends_p(s, q):
        return s < 3 or (s == 3 and q < NQ // 2)

    def sends_m(s, q):
        return s < 3 or (s == 3 and q >= NQ // 2)

    events = []

    def ev_y(q):
        @pl.when(dy == 0)
        def _():
            for i in range(q * QD // PIECE, (q + 1) * QD // PIECE):
                @pl.when(me8 == i)
                def _():
                    own_shard().wait()

                @pl.when(me8 != i)
                def _():
                    p_wait(i)
            y_copy(q, up_y).start()
            remote(chunk(0, q), chunk(0, q), y_send.at[NQ + q], y_recv.at[q], down_y).start()

        @pl.when(dy != 0)
        def _():
            y_copy(q, up_y).wait_recv()

        @pl.when((dy >= 1) & (dy <= 3))
        def _():
            y_copy(q, up_y).start()

        @pl.when(dy >= 6)
        def _():
            y_copy(q, down_y).start()

        zp(0, q).start()
        zm(0, q).start()

    def ev_zp(s, q):
        zp(s, q).wait_recv()
        if sends_p(s + 1, q):
            zp(s + 1, q).start()

    def ev_zm(s, q):
        zm(s, q).wait_recv()
        if sends_m(s + 1, q):
            zm(s + 1, q).start()

    def ev_right(i):
        x_right(i).wait_recv()
        sib(1, i).start()
        if i < NR // 2:
            f_right(i).start()

    def f_left_copy(i):
        return remote(rows(xbuf.at[3, 0], i), rows(xbuf.at[2, 0], i), xl_send.at[NR + i], xl_recv.at[NR + i], left)

    def ev_left(i):
        x_left(i).wait_recv()
        sib(3, i).start()
        if i >= NR // 2:
            f_left_copy(i).start()

    def ev_opp_right(i):
        f_right(i).wait_recv()
        sib(2, i).start()

    def ev_opp_left(i):
        f_left_copy(i).wait_recv()
        sib(2, i).start()

    wt = 2.15 * QD / 128
    xt = 11.5 * RC / 32
    for q in range(NQ):
        events.append((9 + wt * q, ev_y, (q,)))
    n = 0
    for s in range(4):
        for q in range(NQ):
            if sends_p(s, q):
                events.append((11 + wt * (n + 1), ev_zp, (s, q)))
                n += 1
    n = 0
    for s in range(4):
        for q in range(NQ):
            if sends_m(s, q):
                events.append((11 + wt * (n + 1), ev_zm, (s, q)))
                n += 1
    for i in range(NR):
        events.append((4 + xt * (i + 1), ev_right, (i,)))
        events.append((4 + xt * (i + 1), ev_left, (NR - 1 - i,)))
    for i in range(NR // 2):
        events.append((4 + xt * (NR + i + 1), ev_opp_right, (i,)))
        events.append((4 + xt * (NR + i + 1), ev_opp_left, (NR - 1 - i,)))

    def sib_wait(d):
        for i in range(NR):
            sib(d, i).wait_recv()

    def multiply(ds, sets, first=False):
        for d in ds:
            for s in sets:
                start = pl.multiple_of(lax.rem(z - s + NZ, NZ) * DEPTH, DEPTH)
                for r in range(2):
                    part = jnp.dot(xbuf[d, r, :, pl.ds(start, DEPTH)], wbuf[s],
                                   preferred_element_type=jnp.float32)
                    if first and s == sets[0]:
                        acc[d, r] = part
                    else:
                        acc[d, r] += part

    def stage_a():
        own.wait()
        sib_wait(0)
        multiply((0,), (0, 1, 7), True)

    def stage_b():
        sib_wait(1)
        sib_wait(3)
        multiply((1, 3), (0, 1, 7), True)
        multiply((0, 1, 3), (2, 6))

    def stage_c():
        multiply((0, 1, 3), (3, 5))

    events.append((11 + wt * 2 * NQ + 0.5, stage_a, ()))
    events.append((11 + wt * 3 * NQ + 0.6, stage_b, ()))
    events.append((11 + wt * 3.5 * NQ - wt, stage_c, ()))
    events.sort(key=lambda e: e[0])

    for _, go, given in events:
        go(*given)
    sib_wait(2)
    multiply((0, 1, 3), (4,))
    multiply((2,), tuple(range(8)), True)

    done = pltpu.make_async_copy(acc, out_ref, out_sem.at[0])
    done.start()

    @pl.when(dy != 0)
    def _():
        shard_copy().wait_send()

    for q in range(NQ):
        @pl.when((dy <= 3) | (dy >= 6))
        def _():
            y_copy(q, up_y).wait_send()

        @pl.when(dy == 0)
        def _():
            remote(chunk(0, q), chunk(0, q), y_send.at[NQ + q], y_recv.at[q], down_y).wait_send()
    for s in range(4):
        for q in range(NQ):
            if sends_p(s, q):
                zp(s, q).wait_send()
            if sends_m(s, q):
                zm(s, q).wait_send()
    for i in range(NR):
        x_right(i).wait_send()
        x_left(i).wait_send()
        for d in range(4):
            sib(d, i).wait_send()
    for i in range(NR // 2):
        f_right(i).wait_send()
        f_left_copy(NR - 1 - i).wait_send()
    done.wait()


def group_logits(rows, shard):
    dma = pltpu.SemaphoreType.DMA
    return pl.pallas_call(
        kernel,
        out_shape=jax.ShapeDtypeStruct((4, 2, ROWS, COLS), jnp.float32),
        in_specs=[pl.BlockSpec(memory_space=pl.ANY)] * 2,
        out_specs=pl.BlockSpec(memory_space=pl.ANY),
        scratch_shapes=[
            pltpu.VMEM((4, 2, ROWS, FEATURES), jnp.bfloat16),
            pltpu.VMEM((NZ, DEPTH, COLS), jnp.bfloat16),
            pltpu.VMEM((4, 2, ROWS, COLS), jnp.float32),
            dma((2 * NQ,)), dma((NQ,)), dma((1,)), dma((8,)), dma((1,)),
            dma((4, NQ)), dma((4, NQ)), dma((4, NQ)), dma((4, NQ)),
            dma((2 * NR,)), dma((2 * NR,)), dma((2 * NR,)), dma((2 * NR,)),
            dma((4, NR)), dma((4, NR)), dma((1,)), dma((1,)),
        ],
        compiler_params=pltpu.CompilerParams(
            collective_id=0, has_side_effects=True, vmem_limit_bytes=48 * 2**20),
        cost_estimate=pl.CostEstimate(flops=2 * 1024 * COLS * FEATURES, bytes_accessed=8 * 2**20, transcendentals=0),
    )(rows, shard)


def body(rollout_rows, counts, targets, final_gain, lm_head):
    y = lax.axis_index("pipe")
    dp = lax.axis_index("dp")
    c, x, z = dp % 2, (dp // 2) % NX, dp // (2 * NX)
    widened = rollout_rows[0, 0].astype(jnp.float32)
    scaling = lax.rsqrt(jnp.mean(widened * widened, axis=-1, keepdims=True) + 1e-06)
    normed = (widened * scaling * final_gain).astype(jnp.bfloat16).reshape(ROWS, FEATURES)

    learner_counts = counts[0, 0]
    owners = learner_counts.shape[0]
    ids = jnp.arange(owners, dtype=jnp.int32)
    starts = jnp.sum(jnp.where(ids[None, :] < ids[:, None], learner_counts[None, :], 0), axis=1)
    slot = jnp.arange(2, dtype=jnp.int32)
    place = jnp.where(slot[None, :] < learner_counts[:, None], starts[:, None] + slot[None, :], -1).reshape(-1)
    batch_rows = targets.shape[-1]
    hit = place[:, None] == jnp.arange(batch_rows, dtype=jnp.int32)[None, :]
    mine = lax.dynamic_index_in_dim(targets[0], y, 0, keepdims=False)
    slot_targets = jnp.sum(jnp.where(hit, mine[None, :], 0), axis=1).reshape(owners, 2)
    all_targets = lax.all_gather(slot_targets, "dp", axis=0, tiled=False)

    logits = group_logits(normed, lm_head)

    near = lax.dynamic_slice_in_dim(all_targets, z * 8, 8, axis=1)
    ox = (x + jnp.array([0, 3, 2, 1], jnp.int32)) % NX
    oc = jnp.array([0, 1], jnp.int32) ^ c
    order = (ox[:, None] * 2 + oc[None, :]).reshape(-1)
    pick = (order[:, None] == jnp.arange(8)[None, :]).astype(jnp.int32)
    wanted = jnp.sum(jnp.where(pick[:, None, :, None] == 1, near[None], 0), axis=2).reshape(4, 2, ROWS)
    first_column = (dp % 8) * COLS
    column_ids = first_column + lax.broadcasted_iota(jnp.int32, logits.shape, 3)
    largest = jnp.max(logits, axis=-1)
    exp_total = jnp.sum(jnp.exp(logits - largest[..., None]), axis=-1)
    target_logit = jnp.sum(jnp.where(column_ids == wanted[..., None], logits, 0.0), axis=-1)
    stats = jnp.stack([largest, exp_total, target_logit])
    stats = stats.reshape(3, 8, owners, 2)
    stats = jnp.sum(jnp.where(pick[None, :, :, None, None] == 1, stats[:, :, None], 0.0), axis=1)
    sent = stats.transpose(2, 1, 3, 0).reshape(owners, 48)
    got = lax.all_to_all(sent, "dp", split_axis=0, concat_axis=0, tiled=True)
    got = got.reshape(NZ, 8, 8, 2, 3)
    top = jnp.max(got[..., 0], axis=1)
    total = jnp.sum(got[..., 1] * jnp.exp(got[..., 0] - top[:, None]), axis=1)
    picked = jnp.sum(got[..., 2], axis=1)
    slot_log_probs = (picked - (top + jnp.log(total))).reshape(-1)
    log_probs = jnp.sum(jnp.where(hit, slot_log_probs[:, None], 0.0), axis=0)
    return log_probs.reshape(1, 1, batch_rows)


def solution(mesh):
    in_specs = (
        P("pipe", "dp", None, None, None),
        P("pipe", "dp", None),
        P("dp", None, None),
        P(),
        P("dp", "pipe"),
    )
    out_specs = P("pipe", "dp", None)
    return jax.shard_map(body, mesh=mesh, in_specs=in_specs, out_specs=out_specs, check_vma=False)
```

```python
import jax
import jax.numpy as jnp
from jax import lax
from jax.experimental import pallas as pl
from jax.experimental.pallas import tpu as pltpu
from jax.sharding import PartitionSpec as P

NX, NY, NZ, NC = 4, 8, 8, 2
ROWS = 128
FEATURES = 8192
COLS = 384
DEPTH = FEATURES // NZ
PIECE = 128
NQ = 4
QD = DEPTH // NQ
NR = 4
RC = ROWS // NR
MESH = pl.DeviceIdType.MESH


def kernel(x_in, w_in, counts_ref, targets_ref, gain_ref, out_ref, raw, xbuf, wbuf, acc,
           messages, near_targets, ring_targets, hits, wanted, turned, stats, ring_stats, slot_out, slot_in,
           raw_sem, m_send, m_recv, t_send, t_recv, st_send, st_recv, lp_send, lp_recv, y_send, y_recv, p_send, p_recv, p_own,
           zp_send, zp_recv, zm_send, zm_recv, xr_send, xr_recv, xl_send, xl_recv,
           s_send, s_recv):
    y = lax.axis_index("pipe")
    dp = lax.axis_index("dp")
    c = lax.rem(dp, 2)
    x = lax.rem(dp // 2, NX)
    z = dp // (2 * NX)

    def at(zz, xx, cc):
        return (zz * NX + xx) * 2 + cc

    right = (y, at(z, lax.rem(x + 1, NX), c))
    left = (y, at(z, lax.rem(x + NX - 1, NX), c))
    sibling = (y, at(z, x, 1 - c))
    up_z = (y, at(lax.rem(z + 1, NZ), x, c))
    down_z = (y, at(lax.rem(z + NZ - 1, NZ), x, c))
    up_y = (lax.rem(y + 1, NY), dp)
    down_y = (lax.rem(y + NY - 1, NY), dp)
    root_dp = z * 8 + y
    me8 = lax.rem(dp, 8)
    dy = lax.rem(y - me8 + NY, NY)

    def raw_copy(i):
        return pltpu.make_async_copy(rows(x_in, i), rows(raw, i), raw_sem.at[i])

    def rows(ref, i):
        return ref.at[pl.ds(i * RC, RC)]

    for i in range(NR):
        raw_copy(i).start()

    barrier = pltpu.get_barrier_semaphore()
    for step in range(1, 8):
        pl.semaphore_signal(barrier, inc=1, device_id=(y, z * 8 + lax.rem(me8 + step, 8)), device_id_type=MESH)
        pl.semaphore_signal(barrier, inc=1, device_id=(y, lax.rem(dp + 8 * step, 64)), device_id_type=MESH)
    for other in (up_y, down_y):
        pl.semaphore_signal(barrier, inc=1, device_id=other, device_id_type=MESH)
    pl.semaphore_wait(barrier, 16)

    def remote(src, dst, send, recv, device):
        return pltpu.make_async_remote_copy(
            src_ref=src, dst_ref=dst, send_sem=send, recv_sem=recv, device_id=device, device_id_type=MESH)

    def shard_copy():
        return remote(w_in, wbuf.at[0, pl.ds(pl.multiple_of(me8 * PIECE, PIECE), PIECE)],
                      p_send.at[0], p_recv.at[me8], (y, root_dp))

    @pl.when(dy != 0)
    def _():
        shard_copy().start()

    def own_shard():
        return pltpu.make_async_copy(
            w_in, wbuf.at[0, pl.ds(pl.multiple_of(me8 * PIECE, PIECE), PIECE)], p_own.at[0])

    @pl.when(dy == 0)
    def _():
        own_shard().start()

    def x_right(i):
        return remote(rows(xbuf.at[0, 0], i), rows(xbuf.at[1, 0], i), xr_send.at[i], xr_recv.at[i], right)

    def x_left(i):
        return remote(rows(xbuf.at[0, 0], i), rows(xbuf.at[3, 0], i), xl_send.at[i], xl_recv.at[i], left)

    def f_right(i):
        return remote(rows(xbuf.at[1, 0], i), rows(xbuf.at[2, 0], i), xr_send.at[NR + i], xr_recv.at[NR + i], right)

    def sib(d, i):
        return remote(rows(xbuf.at[d, 0], i), rows(xbuf.at[d, 1], i), s_send.at[d, i], s_recv.at[d, i], sibling)

    def normalise(i):
        for b in range(i * RC, (i + 1) * RC, 16):
            here = pl.ds(b, 16)

            def add(j, total):
                v = raw[here, pl.ds(pl.multiple_of(j * 1024, 1024), 1024)].astype(jnp.float32)
                v = v * v
                for n in range(8):
                    total = total + v[:, n * 128:(n + 1) * 128]
                return total

            total = lax.fori_loop(0, FEATURES // 1024, add, jnp.zeros((16, 128), jnp.float32))
            scaling = lax.rsqrt(jnp.sum(total, axis=-1, keepdims=True) / FEATURES + 1e-06)

            def put(j, carry):
                lanes = pl.ds(pl.multiple_of(j * 1024, 1024), 1024)
                v = raw[here, lanes].astype(jnp.float32)
                xbuf[0, 0, here, lanes] = (v * scaling * gain_ref[:, lanes]).astype(jnp.bfloat16)
                return carry

            lax.fori_loop(0, FEATURES // 1024, put, 0)

    for n in range(NR // 2):
        for i in (n, NR - 1 - n):
            raw_copy(i).wait()
            normalise(i)
        x_right(n).start()
        x_left(NR - 1 - n).start()
    for n in range(NR // 2, NR):
        x_right(n).start()
        x_left(NR - 1 - n).start()
    for i in range(NR):
        sib(0, i).start()

    def m_copy(j):
        return remote(messages.at[lax.rem(z + j, NZ)], near_targets.at[j], m_send.at[j], m_recv.at[j],
                      (y, lax.rem(dp + 8 * j, 64)))

    def ring(j):
        return (y, z * 8 + lax.rem(me8 + j, 8))

    def t_copy(j):
        return remote(ring_targets.at[0], ring_targets.at[j], t_send.at[j], t_recv.at[j], ring(j))

    def ev_targets():
        held = counts_ref[...].astype(jnp.float32)
        mine = targets_ref[0, pl.ds(y, 1), :].astype(jnp.float32)
        lane = lax.broadcasted_iota(jnp.int32, (64, 64), 1)
        row = lax.broadcasted_iota(jnp.int32, (64, 64), 0)
        start = jnp.sum(jnp.where(lane < row, held, 0.0), axis=1, keepdims=True)
        number = jnp.sum(jnp.where(lane == row, held, 0.0), axis=1, keepdims=True)
        place = lax.broadcasted_iota(jnp.int32, (64, 128), 1)
        made = jnp.zeros((64, 128), jnp.float32)
        for k in range(2):
            at_row = jnp.where(number > k, start + k, -1.0)
            hit = lane.astype(jnp.float32) == at_row
            hits[k] = jnp.where(hit, 1.0, 0.0)
            target = jnp.sum(jnp.where(hit, mine, 0.0), axis=1, keepdims=True)
            made = made + jnp.where(place == 2 * dp + k, target, 0.0)
        messages[...] = made.reshape(NZ, 8, 128)
        for j in range(1, 8):
            m_copy(j).start()

    def ev_near():
        total = messages[z]
        for j in range(1, 8):
            m_copy(j).wait_recv()
            total = total + near_targets[j]
        ring_targets[0] = total
        for j in range(1, 8):
            t_copy(j).start()

    def owner_of(d, r):
        return lax.rem(x + (NX - d), NX) * 2 + (c if r == 0 else 1 - c)

    def ev_wanted():
        total = ring_targets[0]
        for j in range(1, 8):
            t_copy(j).wait_recv()
            total = total + ring_targets[j]
        wanted[...] = total
        turned[...] = jnp.zeros((128, 128), jnp.float32)
        for d in range(4):
            for r in range(2):
                turned[2 * d + r:2 * d + r + 1, :] = wanted[pl.ds(owner_of(d, r), 1), :]
        turned[...] = turned[...].T

    def chunk(s, q):
        return wbuf.at[s, pl.ds(q * QD, QD)]

    def y_copy(q, device):
        return remote(chunk(0, q), chunk(0, q), y_send.at[q], y_recv.at[q], device)

    def zp(s, q):
        return remote(chunk(s, q), chunk(s + 1, q), zp_send.at[s, q], zp_recv.at[s, q], up_z)

    def zm(s, q):
        return remote(chunk((8 - s) % 8, q), chunk(7 - s, q), zm_send.at[s, q], zm_recv.at[s, q], down_z)

    def p_wait(i):
        remote(w_in, wbuf.at[0, pl.ds(i * PIECE, PIECE)], p_send.at[0], p_recv.at[i], right).wait_recv()

    def sends_p(s, q):
        return s < 3 or (s == 3 and q < NQ // 2)

    def sends_m(s, q):
        return s < 3 or (s == 3 and q >= NQ // 2)

    events = []

    def ev_y(q):
        @pl.when(dy == 0)
        def _():
            for i in range(q * QD // PIECE, (q + 1) * QD // PIECE):
                @pl.when(me8 == i)
                def _():
                    own_shard().wait()

                @pl.when(me8 != i)
                def _():
                    p_wait(i)
            y_copy(q, up_y).start()
            remote(chunk(0, q), chunk(0, q), y_send.at[NQ + q], y_recv.at[q], down_y).start()

        @pl.when(dy != 0)
        def _():
            y_copy(q, up_y).wait_recv()

        @pl.when((dy >= 1) & (dy <= 3))
        def _():
            y_copy(q, up_y).start()

        @pl.when(dy >= 6)
        def _():
            y_copy(q, down_y).start()

        zp(0, q).start()
        zm(0, q).start()

    def ev_zp(s, q):
        zp(s, q).wait_recv()
        if sends_p(s + 1, q):
            zp(s + 1, q).start()

    def ev_zm(s, q):
        zm(s, q).wait_recv()
        if sends_m(s + 1, q):
            zm(s + 1, q).start()

    def ev_right(i):
        x_right(i).wait_recv()
        sib(1, i).start()
        if i < NR // 2:
            f_right(i).start()

    def f_left_copy(i):
        return remote(rows(xbuf.at[3, 0], i), rows(xbuf.at[2, 0], i), xl_send.at[NR + i], xl_recv.at[NR + i], left)

    def ev_left(i):
        x_left(i).wait_recv()
        sib(3, i).start()
        if i >= NR // 2:
            f_left_copy(i).start()

    def ev_opp_right(i):
        f_right(i).wait_recv()
        sib(2, i).start()

    def ev_opp_left(i):
        f_left_copy(i).wait_recv()
        sib(2, i).start()

    wt = 2.15 * QD / 128
    xt = 11.5 * RC / 32
    for q in range(NQ):
        events.append((9 + wt * q, ev_y, (q,)))
    n = 0
    for s in range(4):
        for q in range(NQ):
            if sends_p(s, q):
                events.append((11 + wt * (n + 1), ev_zp, (s, q)))
                n += 1
    n = 0
    for s in range(4):
        for q in range(NQ):
            if sends_m(s, q):
                events.append((11 + wt * (n + 1), ev_zm, (s, q)))
                n += 1
    for i in range(NR):
        events.append((4 + xt * (i + 1), ev_right, (i,)))
        events.append((4 + xt * (i + 1), ev_left, (NR - 1 - i,)))
    for i in range(NR // 2):
        events.append((4 + xt * (NR + i + 1), ev_opp_right, (i,)))
        events.append((4 + xt * (NR + i + 1), ev_opp_left, (NR - 1 - i,)))

    def sib_wait(d):
        for i in range(NR):
            sib(d, i).wait_recv()

    def multiply(ds, sets, first=False):
        for d in ds:
            for s in sets:
                start = pl.multiple_of(lax.rem(z - s + NZ, NZ) * DEPTH, DEPTH)
                for r in range(2):
                    part = jnp.dot(xbuf[d, r, :, pl.ds(start, DEPTH)], wbuf[s],
                                   preferred_element_type=jnp.float32)
                    if first and s == sets[0]:
                        acc[d, r] = part
                    else:
                        acc[d, r] += part

    def stage_a():
        sib_wait(0)
        multiply((0,), (0, 1, 7), True)

    def stage_b():
        sib_wait(1)
        sib_wait(3)
        multiply((1, 3), (0, 1, 7), True)
        multiply((0, 1, 3), (2, 6))

    def stage_c():
        multiply((0, 1, 3), (3, 5))

    events.append((11 + wt * 2 * NQ + 0.5, stage_a, ()))
    events.append((11 + wt * 3 * NQ + 0.6, stage_b, ()))
    events.append((11 + wt * 3.5 * NQ - wt, stage_c, ()))
    events += [(6, ev_targets, ()), (16, ev_near, ()), (22, ev_wanted, ())]
    events.sort(key=lambda e: e[0])

    for _, go, given in events:
        go(*given)
    sib_wait(2)
    multiply((0, 1, 3), (4,))
    multiply((2,), tuple(range(8)), True)

    column = (lax.broadcasted_iota(jnp.int32, (ROWS, COLS), 1) + me8 * COLS).astype(jnp.float32)
    place = lax.broadcasted_iota(jnp.int32, (ROWS, 128), 1)
    gathered = jnp.zeros((ROWS, 128), jnp.float32)
    for d in range(4):
        for r in range(2):
            n = 2 * d + r
            logits = acc[d, r]
            largest = jnp.max(logits, axis=1, keepdims=True)
            exp_total = jnp.sum(jnp.exp(logits - largest), axis=1, keepdims=True)
            target = jnp.sum(jnp.where(column == turned[:, n:n + 1], logits, 0.0), axis=1, keepdims=True)
            for which, v in enumerate((largest, exp_total, target)):
                gathered = jnp.where(place == 8 * which + n, v, gathered)
    turned[...] = gathered.T
    for d in range(4):
        for r in range(2):
            for which in range(3):
                n = 8 * which + 2 * d + r
                stats[which, pl.ds(owner_of(d, r), 1), :] = turned[n:n + 1, :]

    def st_copy(j):
        return remote(stats, ring_stats.at[j], st_send.at[j], st_recv.at[j], ring(j))

    for j in range(1, 8):
        st_copy(j).start()
    for j in range(1, 8):
        st_copy(j).wait_recv()
    parts = [stats[...]] + [ring_stats[j] for j in range(1, 8)]
    top = parts[0][0]
    for part in parts[1:]:
        top = jnp.maximum(top, part[0])
    total = jnp.zeros((8, 128), jnp.float32)
    picked = jnp.zeros((8, 128), jnp.float32)
    for part in parts:
        total = total + part[1] * jnp.exp(part[0] - top)
        picked = picked + part[2]
    slot_out[...] = picked - (top + jnp.log(total))

    def lp_copy(j):
        return remote(slot_out, slot_in.at[z], lp_send.at[j], lp_recv.at[j], (y, lax.rem(dp + 8 * j, 64)))

    for j in range(1, 8):
        lp_copy(j).start()
    slot_in[z] = slot_out[...]
    for j in range(1, 8):
        source = lax.rem(z + NZ - j, NZ)
        remote(slot_out, slot_in.at[source], lp_send.at[j], lp_recv.at[j], up_z).wait_recv()
    slots = slot_in[...].reshape(64, 128)
    result = jnp.zeros((1, 64), jnp.float32)
    for k in range(2):
        value = jnp.sum(jnp.where(place[:64] == 2 * dp + k, slots, 0.0), axis=1, keepdims=True)
        result = result + jnp.sum(jnp.where(hits[k] > 0.5, value, 0.0), axis=0, keepdims=True)
    out_ref[...] = result

    @pl.when(dy != 0)
    def _():
        shard_copy().wait_send()

    for q in range(NQ):
        @pl.when((dy <= 3) | (dy >= 6))
        def _():
            y_copy(q, up_y).wait_send()

        @pl.when(dy == 0)
        def _():
            remote(chunk(0, q), chunk(0, q), y_send.at[NQ + q], y_recv.at[q], down_y).wait_send()
    for s in range(4):
        for q in range(NQ):
            if sends_p(s, q):
                zp(s, q).wait_send()
            if sends_m(s, q):
                zm(s, q).wait_send()
    for i in range(NR):
        x_right(i).wait_send()
        x_left(i).wait_send()
        for d in range(4):
            sib(d, i).wait_send()
    for i in range(NR // 2):
        f_right(i).wait_send()
        f_left_copy(NR - 1 - i).wait_send()
    for j in range(1, 8):
        m_copy(j).wait_send()
        t_copy(j).wait_send()
        st_copy(j).wait_send()
        lp_copy(j).wait_send()


def body(rollout_rows, counts, targets, final_gain, lm_head):
    rows = lax.optimization_barrier(rollout_rows.reshape(ROWS, FEATURES))
    dma = pltpu.SemaphoreType.DMA
    vmem = pl.BlockSpec(memory_space=pltpu.VMEM)
    hbm = pl.BlockSpec(memory_space=pl.ANY)
    tile = (8, 128)
    f32 = jnp.float32
    log_probs = pl.pallas_call(
        kernel,
        out_shape=jax.ShapeDtypeStruct((1, 64), f32),
        in_specs=[hbm, hbm, vmem, vmem, vmem],
        out_specs=vmem,
        scratch_shapes=[
            pltpu.VMEM((ROWS, FEATURES), jnp.bfloat16),
            pltpu.VMEM((4, 2, ROWS, FEATURES), jnp.bfloat16),
            pltpu.VMEM((NZ, DEPTH, COLS), jnp.bfloat16),
            pltpu.VMEM((4, 2, ROWS, COLS), f32),
            pltpu.VMEM((NZ, *tile), f32), pltpu.VMEM((NZ, *tile), f32), pltpu.VMEM((8, *tile), f32),
            pltpu.VMEM((2, 64, 64), f32), pltpu.VMEM(tile, f32), pltpu.VMEM((128, 128), f32),
            pltpu.VMEM((3, *tile), f32), pltpu.VMEM((8, 3, *tile), f32),
            pltpu.VMEM(tile, f32), pltpu.VMEM((NZ, *tile), f32),
            dma((NR,)), dma((8,)), dma((8,)), dma((8,)), dma((8,)), dma((8,)), dma((8,)), dma((8,)), dma((8,)),
            dma((2 * NQ,)), dma((NQ,)), dma((1,)), dma((8,)), dma((1,)),
            dma((4, NQ)), dma((4, NQ)), dma((4, NQ)), dma((4, NQ)),
            dma((2 * NR,)), dma((2 * NR,)), dma((2 * NR,)), dma((2 * NR,)),
            dma((4, NR)), dma((4, NR)),
        ],
        compiler_params=pltpu.CompilerParams(
            collective_id=0, has_side_effects=True, vmem_limit_bytes=48 * 2**20),
        cost_estimate=pl.CostEstimate(flops=2 * 1024 * COLS * FEATURES, bytes_accessed=8 * 2**20, transcendentals=0),
    )(rows, lm_head, counts[0], targets, final_gain.reshape(1, FEATURES))
    return log_probs.reshape(1, 1, 64)


def solution(mesh):
    in_specs = (
        P("pipe", "dp", None, None, None),
        P("pipe", "dp", None),
        P("dp", None, None),
        P(),
        P("dp", "pipe"),
    )
    out_specs = P("pipe", "dp", None)
    return jax.shard_map(body, mesh=mesh, in_specs=in_specs, out_specs=out_specs, check_vma=False)
```

```python
import jax
import jax.numpy as jnp
from jax import lax
from jax.experimental import pallas as pl
from jax.experimental.pallas import tpu as pltpu
from jax.sharding import PartitionSpec as P

NX, NY, NZ, NC = 4, 8, 8, 2
ROWS = 128
FEATURES = 8192
COLS = 384
DEPTH = FEATURES // NZ
PIECE = 128
NK = 4
PART = COLS // NK
NR = 4
RC = ROWS // NR
MESH = pl.DeviceIdType.MESH


def kernel(x_in, w_in, counts_ref, targets_ref, gain_ref, out_ref, raw, flipped, xbuf, wbuf, acc,
           messages, near_targets, ring_targets, hits, wanted, turned, noted, stats, ring_stats, slot_out, slot_in,
           raw_sem, m_send, m_recv, t_send, t_recv, st_send, st_recv, lp_send, lp_recv, y_send, y_recv, p_send, p_recv, p_own,
           zp_send, zp_recv, zm_send, zm_recv, xr_send, xr_recv, xl_send, xl_recv,
           s_send, s_recv):
    y = lax.axis_index("pipe")
    dp = lax.axis_index("dp")
    c = lax.rem(dp, 2)
    x = lax.rem(dp // 2, NX)
    z = dp // (2 * NX)

    def at(zz, xx, cc):
        return (zz * NX + xx) * 2 + cc

    right = (y, at(z, lax.rem(x + 1, NX), c))
    left = (y, at(z, lax.rem(x + NX - 1, NX), c))
    sibling = (y, at(z, x, 1 - c))
    up_z = (y, at(lax.rem(z + 1, NZ), x, c))
    down_z = (y, at(lax.rem(z + NZ - 1, NZ), x, c))
    up_y = (lax.rem(y + 1, NY), dp)
    down_y = (lax.rem(y + NY - 1, NY), dp)
    me8 = lax.rem(dp, 8)
    keeper = lax.rem(y, 2) == c

    def raw_copy(i):
        return pltpu.make_async_copy(rows(x_in, i), rows(raw, i), raw_sem.at[i])

    def rows(ref, i):
        return ref.at[pl.ds(i * RC, RC)]

    for i in range(NR):
        raw_copy(i).start()

    barrier = pltpu.get_barrier_semaphore()
    for step in range(1, 8):
        pl.semaphore_signal(barrier, inc=1, device_id=(y, z * 8 + lax.rem(me8 + step, 8)), device_id_type=MESH)
        pl.semaphore_signal(barrier, inc=1, device_id=(y, lax.rem(dp + 8 * step, 64)), device_id_type=MESH)
    for other in (up_y, down_y):
        pl.semaphore_signal(barrier, inc=1, device_id=other, device_id_type=MESH)
    flipped[...] = w_in[...].astype(jnp.float32).T.astype(jnp.bfloat16)
    pl.semaphore_wait(barrier, 16)

    def remote(src, dst, send, recv, device):
        return pltpu.make_async_remote_copy(
            src_ref=src, dst_ref=dst, send_sem=send, recv_sem=recv, device_id=device, device_id_type=MESH)

    def shard_copy(step):
        other = lax.rem(x + step, NX)
        return remote(flipped.at[pl.ds(pl.multiple_of(other * PART, PART), PART)],
                      wbuf.at[0, pl.ds(0, PART), pl.ds(pl.multiple_of(me8 * PIECE, PIECE), PIECE)],
                      p_send.at[step], p_recv.at[me8], (y, at(z, other, lax.rem(y, 2))))

    def own_shard():
        return pltpu.make_async_copy(
            flipped.at[pl.ds(pl.multiple_of(x * PART, PART), PART)],
            wbuf.at[0, pl.ds(0, PART), pl.ds(pl.multiple_of(me8 * PIECE, PIECE), PIECE)], p_own.at[0])

    for step in (2, 1, 3):
        shard_copy(step).start()

    @pl.when(keeper)
    def _():
        own_shard().start()

    @pl.when(jnp.logical_not(keeper))
    def _():
        shard_copy(0).start()

    def x_right(i):
        return remote(rows(xbuf.at[0, 0], i), rows(xbuf.at[1, 0], i), xr_send.at[i], xr_recv.at[i], right)

    def x_left(i):
        return remote(rows(xbuf.at[0, 0], i), rows(xbuf.at[3, 0], i), xl_send.at[i], xl_recv.at[i], left)

    def f_right(i):
        return remote(rows(xbuf.at[1, 0], i), rows(xbuf.at[2, 0], i), xr_send.at[NR + i], xr_recv.at[NR + i], right)

    def sib(d, i):
        return remote(rows(xbuf.at[d, 0], i), rows(xbuf.at[d, 1], i), s_send.at[d, i], s_recv.at[d, i], sibling)

    def normalise(i):
        for b in range(i * RC, (i + 1) * RC, 16):
            here = pl.ds(b, 16)

            def add(j, total):
                v = raw[here, pl.ds(pl.multiple_of(j * 1024, 1024), 1024)].astype(jnp.float32)
                v = v * v
                for n in range(8):
                    total = total + v[:, n * 128:(n + 1) * 128]
                return total

            total = lax.fori_loop(0, FEATURES // 1024, add, jnp.zeros((16, 128), jnp.float32))
            scaling = lax.rsqrt(jnp.sum(total, axis=-1, keepdims=True) / FEATURES + 1e-06)

            def put(j, carry):
                lanes = pl.ds(pl.multiple_of(j * 1024, 1024), 1024)
                v = raw[here, lanes].astype(jnp.float32)
                xbuf[0, 0, here, lanes] = (v * scaling * gain_ref[:, lanes]).astype(jnp.bfloat16)
                return carry

            lax.fori_loop(0, FEATURES // 1024, put, 0)

    def m_copy(j):
        return remote(messages.at[lax.rem(z + j, NZ)], near_targets.at[j], m_send.at[j], m_recv.at[j],
                      (y, lax.rem(dp + 8 * j, 64)))

    def ring(j):
        return (y, z * 8 + lax.rem(me8 + j, 8))

    def t_copy(j):
        return remote(ring_targets.at[0], ring_targets.at[j], t_send.at[j], t_recv.at[j], ring(j))

    def ev_targets():
        held = counts_ref[...].astype(jnp.float32)
        mine = targets_ref[0, pl.ds(y, 1), :].astype(jnp.float32)
        lane = lax.broadcasted_iota(jnp.int32, (64, 64), 1)
        row = lax.broadcasted_iota(jnp.int32, (64, 64), 0)
        start = jnp.sum(jnp.where(lane < row, held, 0.0), axis=1, keepdims=True)
        number = jnp.sum(jnp.where(lane == row, held, 0.0), axis=1, keepdims=True)
        place = lax.broadcasted_iota(jnp.int32, (64, 128), 1)
        made = jnp.zeros((64, 128), jnp.float32)
        for k in range(2):
            at_row = jnp.where(number > k, start + k, -1.0)
            hit = lane.astype(jnp.float32) == at_row
            hits[k] = jnp.where(hit, 1.0, 0.0)
            target = jnp.sum(jnp.where(hit, mine, 0.0), axis=1, keepdims=True)
            made = made + jnp.where(place == 2 * dp + k, target, 0.0)
        messages[...] = made.reshape(NZ, 8, 128)
        for j in range(1, 8):
            m_copy(j).start()

    def ev_near():
        total = messages[z]
        for j in range(1, 8):
            m_copy(j).wait_recv()
            total = total + near_targets[j]
        ring_targets[0] = total
        for j in range(1, 8):
            t_copy(j).start()

    def owner_of(d, r):
        return lax.rem(x + (NX - d), NX) * 2 + (c if r == 0 else 1 - c)

    def ev_wanted():
        total = ring_targets[0]
        for j in range(1, 8):
            t_copy(j).wait_recv()
            total = total + ring_targets[j]
        wanted[...] = total
        turned[...] = jnp.zeros((128, 128), jnp.float32)
        for d in range(4):
            for r in range(2):
                turned[2 * d + r:2 * d + r + 1, :] = wanted[pl.ds(owner_of(d, r), 1), :]
        turned[...] = turned[...].T

    def chunk(s, r):
        return wbuf.at[s, pl.ds(r * PART, PART)]

    def y_copy(r, to, way):
        return remote(chunk(0, r), chunk(0, to), y_send.at[r, way], y_recv.at[to], (up_y, down_y)[way])

    keeper_sends = (((0, 0, 0), (0, 1, 1)), ((1, 2, 0),), ((2, 3, 1),), ())
    other_sends = (((0, 1, 0),), ((1, 2, 1),), ((2, 3, 0),), ())

    def zp(s, q):
        return remote(chunk(s, q), chunk(s + 1, q), zp_send.at[s, q], zp_recv.at[s, q], up_z)

    def zm(s, q):
        return remote(chunk((8 - s) % 8, q), chunk(7 - s, q), zm_send.at[s, q], zm_recv.at[s, q], down_z)

    def sends_p(s, q):
        return s < 3 or (s == 3 and q < NK // 2)

    def sends_m(s, q):
        return s < 3 or (s == 3 and q >= NK // 2)

    events = []

    def ev_part(r):
        @pl.when(keeper)
        def _():
            if r == 0:
                own_shard().wait()
                for i in range(1, 8):
                    source = lax.rem(me8 + i, 8)
                    remote(flipped.at[pl.ds(0, PART)], wbuf.at[0, pl.ds(0, PART), pl.ds(0, PIECE)],
                           p_send.at[0], p_recv.at[source], right).wait_recv()
            else:
                y_copy(r, r, 0).wait_recv()
            for send in keeper_sends[r]:
                y_copy(*send).start()

        @pl.when(jnp.logical_not(keeper))
        def _():
            y_copy(r, r, 0).wait_recv()
            for send in other_sends[r]:
                y_copy(*send).start()

        zp(0, r).start()
        zm(0, r).start()

    def ev_zp(s, q):
        zp(s, q).wait_recv()
        if sends_p(s + 1, q):
            zp(s + 1, q).start()

    def ev_zm(s, q):
        zm(s, q).wait_recv()
        if sends_m(s + 1, q):
            zm(s + 1, q).start()

    def ev_rows(n):
        x_right(n).start()
        x_left(NR - 1 - n).start()

    def ev_right(i):
        x_right(i).wait_recv()
        sib(1, i).start()
        if i < NR // 2:
            f_right(i).start()

    def f_left_copy(i):
        return remote(rows(xbuf.at[3, 0], i), rows(xbuf.at[2, 0], i), xl_send.at[NR + i], xl_recv.at[NR + i], left)

    def ev_left(i):
        x_left(i).wait_recv()
        sib(3, i).start()
        if i >= NR // 2:
            f_left_copy(i).start()

    def ev_opp_right(i):
        f_right(i).wait_recv()
        sib(2, i).start()

    def ev_opp_left(i):
        f_left_copy(i).wait_recv()
        sib(2, i).start()

    for r, t in enumerate((6, 13, 15, 22)):
        events.append((t, ev_part, (r,)))
    for s, times in enumerate(((14, 18, 24, 29), (33, 37, 41, 45), (50, 54, 58, 62), (66, 67, 68, 69))):
        for q, t in enumerate(times):
            if sends_p(s, q):
                events.append((t, ev_zp, (s, q)))
            if sends_m(s, q):
                events.append((t, ev_zm, (s, q)))
    for i, t in enumerate((25, 34, 45.5, 58.5)):
        events.append((t, ev_right, (i,)))
        events.append((t, ev_left, (NR - 1 - i,)))
    for i, t in enumerate((65.8, 74)):
        events.append((t, ev_opp_right, (i,)))
        events.append((t, ev_opp_left, (NR - 1 - i,)))

    def sib_wait(d):
        for i in range(NR):
            sib(d, i).wait_recv()

    def multiply(ds, sets, first=False):
        for d in ds:
            for s in sets:
                start = pl.multiple_of(lax.rem(z - s + NZ, NZ) * DEPTH, DEPTH)
                for r in range(2):
                    part = lax.dot_general(xbuf[d, r, :, pl.ds(start, DEPTH)], wbuf[s], (((1,), (1,)), ((), ())),
                                           preferred_element_type=jnp.float32)
                    if first and s == sets[0]:
                        acc[d, r] = part
                    else:
                        acc[d, r] += part

    lane = lax.broadcasted_iota(jnp.int32, (1, COLS), 1)
    column = lane
    for r, (kept, other) in enumerate(((0, 7), (6, 1), (2, 5), (4, 3))):
        block = lax.rem(y + jnp.where(keeper, kept, other), NY)
        column = jnp.where(lane >= r * PART, block * COLS + x * PART + lane - r * PART, column)
    column = column.astype(jnp.float32)
    place = lax.broadcasted_iota(jnp.int32, (ROWS, 128), 1)

    def note_statistics(ds, fresh):
        gathered = jnp.zeros((ROWS, 128), jnp.float32) if fresh else noted[...]
        for d in ds:
            for r in range(2):
                n = 2 * d + r
                logits = acc[d, r]
                largest = jnp.max(logits, axis=1, keepdims=True)
                exp_total = jnp.sum(jnp.exp(logits - largest), axis=1, keepdims=True)
                target = jnp.sum(jnp.where(column == turned[:, n:n + 1], logits, 0.0), axis=1, keepdims=True)
                for which, v in enumerate((largest, exp_total, target)):
                    gathered = jnp.where(place == 8 * which + n, v, gathered)
        noted[...] = gathered

    early = (0, 1, 7, 2, 6)

    def stage_a():
        sib_wait(0)
        multiply((0,), early, True)

    def stage_b():
        sib_wait(1)
        sib_wait(3)
        multiply((1, 3), early, True)

    def stage_c():
        multiply((0, 1, 3), (3, 5))

    def stage_d():
        multiply((0, 1, 3), (4,))
        note_statistics((0, 1, 3), True)

    events += [(47, stage_a, ()), (59, stage_b, ()), (64, stage_c, ()), (70, stage_d, ())]
    events += [(5.5, ev_near, ()), (40, ev_wanted, ())]
    events += [(5.6, ev_rows, (n,)) for n in range(NR // 2, NR)]
    events.sort(key=lambda e: e[0])

    ev_targets()
    for n in range(NR // 2):
        for i in (n, NR - 1 - n):
            raw_copy(i).wait()
            normalise(i)
        ev_rows(n)
    for i in range(NR):
        sib(0, i).start()
    for _, go, given in events:
        go(*given)
    sib_wait(2)
    multiply((2,), tuple(range(8)), True)
    note_statistics((2,), False)
    turned[...] = noted[...].T
    for d in range(4):
        for r in range(2):
            for which in range(3):
                n = 8 * which + 2 * d + r
                stats[which, pl.ds(owner_of(d, r), 1), :] = turned[n:n + 1, :]

    def st_copy(j):
        return remote(stats, ring_stats.at[j], st_send.at[j], st_recv.at[j], ring(j))

    for j in range(1, 8):
        st_copy(j).start()
    for j in range(1, 8):
        st_copy(j).wait_recv()
    parts = [stats[...]] + [ring_stats[j] for j in range(1, 8)]
    top = parts[0][0]
    for part in parts[1:]:
        top = jnp.maximum(top, part[0])
    total = jnp.zeros((8, 128), jnp.float32)
    picked = jnp.zeros((8, 128), jnp.float32)
    for part in parts:
        total = total + part[1] * jnp.exp(part[0] - top)
        picked = picked + part[2]
    slot_out[...] = picked - (top + jnp.log(total))

    def lp_copy(j):
        return remote(slot_out, slot_in.at[z], lp_send.at[j], lp_recv.at[j], (y, lax.rem(dp + 8 * j, 64)))

    for j in range(1, 8):
        lp_copy(j).start()
    slot_in[z] = slot_out[...]
    for j in range(1, 8):
        source = lax.rem(z + NZ - j, NZ)
        remote(slot_out, slot_in.at[source], lp_send.at[j], lp_recv.at[j], up_z).wait_recv()
    slots = slot_in[...].reshape(64, 128)
    result = jnp.zeros((1, 64), jnp.float32)
    for k in range(2):
        value = jnp.sum(jnp.where(place[:64] == 2 * dp + k, slots, 0.0), axis=1, keepdims=True)
        result = result + jnp.sum(jnp.where(hits[k] > 0.5, value, 0.0), axis=0, keepdims=True)
    out_ref[...] = result

    for step in (1, 2, 3):
        shard_copy(step).wait_send()

    @pl.when(jnp.logical_not(keeper))
    def _():
        shard_copy(0).wait_send()
        for sends in other_sends:
            for send in sends:
                y_copy(*send).wait_send()

    @pl.when(keeper)
    def _():
        for sends in keeper_sends:
            for send in sends:
                y_copy(*send).wait_send()

    for s in range(4):
        for q in range(NK):
            if sends_p(s, q):
                zp(s, q).wait_send()
            if sends_m(s, q):
                zm(s, q).wait_send()
    for i in range(NR):
        x_right(i).wait_send()
        x_left(i).wait_send()
        for d in range(4):
            sib(d, i).wait_send()
    for i in range(NR // 2):
        f_right(i).wait_send()
        f_left_copy(NR - 1 - i).wait_send()
    for j in range(1, 8):
        m_copy(j).wait_send()
        t_copy(j).wait_send()
        st_copy(j).wait_send()
        lp_copy(j).wait_send()


def body(rollout_rows, counts, targets, final_gain, lm_head):
    rows = lax.optimization_barrier(rollout_rows.reshape(ROWS, FEATURES))
    dma = pltpu.SemaphoreType.DMA
    vmem = pl.BlockSpec(memory_space=pltpu.VMEM)
    hbm = pl.BlockSpec(memory_space=pl.ANY)
    tile = (8, 128)
    f32 = jnp.float32
    log_probs = pl.pallas_call(
        kernel,
        out_shape=jax.ShapeDtypeStruct((1, 64), f32),
        in_specs=[hbm, vmem, vmem, vmem, vmem],
        out_specs=vmem,
        scratch_shapes=[
            pltpu.VMEM((ROWS, FEATURES), jnp.bfloat16),
            pltpu.VMEM((COLS, PIECE), jnp.bfloat16),
            pltpu.VMEM((4, 2, ROWS, FEATURES), jnp.bfloat16),
            pltpu.VMEM((NZ, COLS, DEPTH), jnp.bfloat16),
            pltpu.VMEM((4, 2, ROWS, COLS), f32),
            pltpu.VMEM((NZ, *tile), f32), pltpu.VMEM((NZ, *tile), f32), pltpu.VMEM((8, *tile), f32),
            pltpu.VMEM((2, 64, 64), f32), pltpu.VMEM(tile, f32), pltpu.VMEM((128, 128), f32), pltpu.VMEM((128, 128), f32),
            pltpu.VMEM((3, *tile), f32), pltpu.VMEM((8, 3, *tile), f32),
            pltpu.VMEM(tile, f32), pltpu.VMEM((NZ, *tile), f32),
            dma((NR,)), dma((8,)), dma((8,)), dma((8,)), dma((8,)), dma((8,)), dma((8,)), dma((8,)), dma((8,)),
            dma((NK, 2)), dma((NK,)), dma((4,)), dma((8,)), dma((1,)),
            dma((4, NK)), dma((4, NK)), dma((4, NK)), dma((4, NK)),
            dma((2 * NR,)), dma((2 * NR,)), dma((2 * NR,)), dma((2 * NR,)),
            dma((4, NR)), dma((4, NR)),
        ],
        compiler_params=pltpu.CompilerParams(
            collective_id=0, has_side_effects=True, vmem_limit_bytes=48 * 2**20),
        cost_estimate=pl.CostEstimate(flops=2 * 1024 * COLS * FEATURES, bytes_accessed=8 * 2**20, transcendentals=0),
    )(rows, lm_head, counts[0], targets, final_gain.reshape(1, FEATURES))
    return log_probs.reshape(1, 1, 64)


def solution(mesh):
    in_specs = (
        P("pipe", "dp", None, None, None),
        P("pipe", "dp", None),
        P("dp", None, None),
        P(),
        P("dp", "pipe"),
    )
    out_specs = P("pipe", "dp", None)
    return jax.shard_map(body, mesh=mesh, in_specs=in_specs, out_specs=out_specs, check_vma=False)
```

```python
import jax
import jax.numpy as jnp
from jax import lax
from jax.experimental import pallas as pl
from jax.experimental.pallas import tpu as pltpu
from jax.sharding import PartitionSpec as P

NX, NY, NZ, NC = 4, 8, 8, 2
ROWS = 128
FEATURES = 8192
COLS = 384
DEPTH = FEATURES // NZ
PIECE = 128
NK = 4
PART = COLS // NK
NR = 4
RC = ROWS // NR
MESH = pl.DeviceIdType.MESH


def kernel(x_in, w_in, counts_ref, targets_ref, gain_ref, out_ref, raw, flipped, xbuf, wbuf, acc,
           messages, near_targets, ring_targets, hits, wanted, turned, noted, stats, ring_stats, slot_out, slot_in,
           raw_sem, m_send, m_recv, t_send, t_recv, st_send, st_recv, lp_send, lp_recv, y_send, y_recv, p_send, p_recv, p_own,
           zp_send, zp_recv, zm_send, zm_recv, xr_send, xr_recv, xl_send, xl_recv,
           s_send, s_recv):
    y = lax.axis_index("pipe")
    dp = lax.axis_index("dp")
    c = lax.rem(dp, 2)
    x = lax.rem(dp // 2, NX)
    z = dp // (2 * NX)

    def at(zz, xx, cc):
        return (zz * NX + xx) * 2 + cc

    right = (y, at(z, lax.rem(x + 1, NX), c))
    left = (y, at(z, lax.rem(x + NX - 1, NX), c))
    sibling = (y, at(z, x, 1 - c))
    up_z = (y, at(lax.rem(z + 1, NZ), x, c))
    down_z = (y, at(lax.rem(z + NZ - 1, NZ), x, c))
    up_y = (lax.rem(y + 1, NY), dp)
    down_y = (lax.rem(y + NY - 1, NY), dp)
    me8 = lax.rem(dp, 8)
    keeper = lax.rem(y, 2) == c

    def raw_copy(i):
        return pltpu.make_async_copy(x_in.at[pl.ds(i * RC // 2, RC // 2)], raw.at[pl.ds(i * RC // 2, RC // 2)], raw_sem.at[i])

    def rows(ref, i):
        return ref.at[pl.ds(i * RC, RC)]

    for i in range(NR):
        raw_copy(i).start()

    barrier = pltpu.get_barrier_semaphore()
    for step in range(1, 8):
        pl.semaphore_signal(barrier, inc=1, device_id=(y, z * 8 + lax.rem(me8 + step, 8)), device_id_type=MESH)
        pl.semaphore_signal(barrier, inc=1, device_id=(y, lax.rem(dp + 8 * step, 64)), device_id_type=MESH)
    for other in (up_y, down_y):
        pl.semaphore_signal(barrier, inc=1, device_id=other, device_id_type=MESH)
    flipped[...] = w_in[...].astype(jnp.float32).T.astype(jnp.bfloat16)
    pl.semaphore_wait(barrier, 16)

    def remote(src, dst, send, recv, device):
        return pltpu.make_async_remote_copy(
            src_ref=src, dst_ref=dst, send_sem=send, recv_sem=recv, device_id=device, device_id_type=MESH)

    def shard_copy(step):
        other = lax.rem(x + step, NX)
        return remote(flipped.at[pl.ds(pl.multiple_of(other * PART, PART), PART)],
                      wbuf.at[0, pl.ds(0, PART), pl.ds(pl.multiple_of(me8 * PIECE, PIECE), PIECE)],
                      p_send.at[step], p_recv.at[me8], (y, at(z, other, lax.rem(y, 2))))

    def own_shard():
        return pltpu.make_async_copy(
            flipped.at[pl.ds(pl.multiple_of(x * PART, PART), PART)],
            wbuf.at[0, pl.ds(0, PART), pl.ds(pl.multiple_of(me8 * PIECE, PIECE), PIECE)], p_own.at[0])

    for step in (2, 1, 3):
        shard_copy(step).start()

    @pl.when(keeper)
    def _():
        own_shard().start()

    @pl.when(jnp.logical_not(keeper))
    def _():
        shard_copy(0).start()

    def x_right(i):
        return remote(rows(xbuf.at[0, 0], i), rows(xbuf.at[1, 0], i), xr_send.at[i], xr_recv.at[i], right)

    def x_left(i):
        return remote(rows(xbuf.at[0, 0], i), rows(xbuf.at[3, 0], i), xl_send.at[i], xl_recv.at[i], left)

    def f_right(i):
        return remote(rows(xbuf.at[1, 0], i), rows(xbuf.at[2, 0], i), xr_send.at[NR + i], xr_recv.at[NR + i], right)

    def sib(d, i):
        return remote(rows(xbuf.at[d, 0], i), rows(xbuf.at[d, 1], i), s_send.at[d, i], s_recv.at[d, i], sibling)

    def normalise(i):
        for b in range(i * RC, (i + 1) * RC, 16):
            here = pl.ds(b, 16)
            pairs = pl.ds(b // 2, 8)

            def add(j, total):
                lanes = pl.ds(pl.multiple_of(j * 1024, 1024), 1024)
                v = raw[pairs, :, lanes].reshape(16, 1024)
                xbuf[0, 0, here, lanes] = v
                v = v.astype(jnp.float32)
                v = v * v
                for n in range(8):
                    total = total + v[:, n * 128:(n + 1) * 128]
                return total

            total = lax.fori_loop(0, FEATURES // 1024, add, jnp.zeros((16, 128), jnp.float32))
            scaling = lax.rsqrt(jnp.sum(total, axis=-1, keepdims=True) / FEATURES + 1e-06)

            def put(j, carry):
                lanes = pl.ds(pl.multiple_of(j * 1024, 1024), 1024)
                v = xbuf[0, 0, here, lanes].astype(jnp.float32)
                xbuf[0, 0, here, lanes] = (v * scaling * gain_ref[:, lanes]).astype(jnp.bfloat16)
                return carry

            lax.fori_loop(0, FEATURES // 1024, put, 0)

    def m_copy(j):
        return remote(messages.at[lax.rem(z + j, NZ)], near_targets.at[j], m_send.at[j], m_recv.at[j],
                      (y, lax.rem(dp + 8 * j, 64)))

    def ring(j):
        return (y, z * 8 + lax.rem(me8 + j, 8))

    def t_copy(j):
        return remote(ring_targets.at[0], ring_targets.at[j], t_send.at[j], t_recv.at[j], ring(j))

    def ev_targets():
        held = counts_ref[...].astype(jnp.float32)
        mine = targets_ref[0, pl.ds(y, 1), :].astype(jnp.float32)
        lane = lax.broadcasted_iota(jnp.int32, (64, 64), 1)
        row = lax.broadcasted_iota(jnp.int32, (64, 64), 0)
        start = jnp.sum(jnp.where(lane < row, held, 0.0), axis=1, keepdims=True)
        number = jnp.sum(jnp.where(lane == row, held, 0.0), axis=1, keepdims=True)
        place = lax.broadcasted_iota(jnp.int32, (64, 128), 1)
        made = jnp.zeros((64, 128), jnp.float32)
        for k in range(2):
            at_row = jnp.where(number > k, start + k, -1.0)
            hit = lane.astype(jnp.float32) == at_row
            hits[k] = jnp.where(hit, 1.0, 0.0)
            target = jnp.sum(jnp.where(hit, mine, 0.0), axis=1, keepdims=True)
            made = made + jnp.where(place == 2 * dp + k, target, 0.0)
        messages[...] = made.reshape(NZ, 8, 128)
        for j in range(1, 8):
            m_copy(j).start()

    def ev_near():
        total = messages[z]
        for j in range(1, 8):
            m_copy(j).wait_recv()
            total = total + near_targets[j]
        ring_targets[0] = total
        for j in range(1, 8):
            t_copy(j).start()

    def owner_of(d, r):
        return lax.rem(x + (NX - d), NX) * 2 + (c if r == 0 else 1 - c)

    def ev_wanted():
        total = ring_targets[0]
        for j in range(1, 8):
            t_copy(j).wait_recv()
            total = total + ring_targets[j]
        wanted[...] = total
        turned[...] = jnp.zeros((128, 128), jnp.float32)
        for d in range(4):
            for r in range(2):
                turned[2 * d + r:2 * d + r + 1, :] = wanted[pl.ds(owner_of(d, r), 1), :]
        turned[...] = turned[...].T

    def chunk(s, r):
        return wbuf.at[s, pl.ds(r * PART, PART)]

    def y_copy(r, to, way):
        return remote(chunk(0, r), chunk(0, to), y_send.at[r, way], y_recv.at[to], (up_y, down_y)[way])

    keeper_sends = (((0, 0, 0), (0, 1, 1)), ((1, 2, 0),), ((2, 3, 1),), ())
    other_sends = (((0, 1, 0),), ((1, 2, 1),), ((2, 3, 0),), ())

    def zp(s, q):
        return remote(chunk(s, q), chunk(s + 1, q), zp_send.at[s, q], zp_recv.at[s, q], up_z)

    def zm(s, q):
        return remote(chunk((8 - s) % 8, q), chunk(7 - s, q), zm_send.at[s, q], zm_recv.at[s, q], down_z)

    def sends_p(s, q):
        return s < 3 or (s == 3 and q < NK // 2)

    def sends_m(s, q):
        return s < 3 or (s == 3 and q >= NK // 2)

    events = []

    def ev_part(r):
        @pl.when(keeper)
        def _():
            if r == 0:
                own_shard().wait()
                for i in range(1, 8):
                    source = lax.rem(me8 + i, 8)
                    remote(flipped.at[pl.ds(0, PART)], wbuf.at[0, pl.ds(0, PART), pl.ds(0, PIECE)],
                           p_send.at[0], p_recv.at[source], right).wait_recv()
            else:
                y_copy(r, r, 0).wait_recv()
            for send in keeper_sends[r]:
                y_copy(*send).start()

        @pl.when(jnp.logical_not(keeper))
        def _():
            y_copy(r, r, 0).wait_recv()
            for send in other_sends[r]:
                y_copy(*send).start()

        zp(0, r).start()
        zm(0, r).start()

    def ev_zp(s, q):
        zp(s, q).wait_recv()
        if sends_p(s + 1, q):
            zp(s + 1, q).start()

    def ev_zm(s, q):
        zm(s, q).wait_recv()
        if sends_m(s + 1, q):
            zm(s + 1, q).start()

    def ev_rows(n):
        x_right(n).start()
        x_left(NR - 1 - n).start()

    def ev_right(i):
        x_right(i).wait_recv()
        sib(1, i).start()
        if i < NR // 2:
            f_right(i).start()

    def f_left_copy(i):
        return remote(rows(xbuf.at[3, 0], i), rows(xbuf.at[2, 0], i), xl_send.at[NR + i], xl_recv.at[NR + i], left)

    def ev_left(i):
        x_left(i).wait_recv()
        sib(3, i).start()
        if i >= NR // 2:
            f_left_copy(i).start()

    def ev_opp_right(i):
        f_right(i).wait_recv()
        sib(2, i).start()

    def ev_opp_left(i):
        f_left_copy(i).wait_recv()
        sib(2, i).start()

    for r, t in enumerate((6, 13, 15, 22)):
        events.append((t, ev_part, (r,)))
    for s, times in enumerate(((14, 18, 24, 29), (33, 37, 41, 45), (50, 54, 58, 62), (66, 67, 68, 69))):
        for q, t in enumerate(times):
            if sends_p(s, q):
                events.append((t, ev_zp, (s, q)))
            if sends_m(s, q):
                events.append((t, ev_zm, (s, q)))
    for i, t in enumerate((25, 34, 45.5, 58.5)):
        events.append((t, ev_right, (i,)))
        events.append((t, ev_left, (NR - 1 - i,)))
    for i, t in enumerate((65.8, 69.5)):
        events.append((t, ev_opp_right, (i,)))
        events.append((t, ev_opp_left, (NR - 1 - i,)))

    def sib_wait(d):
        for i in range(NR):
            sib(d, i).wait_recv()

    def multiply(ds, sets, first=False):
        for d in ds:
            for s in sets:
                start = pl.multiple_of(lax.rem(z - s + NZ, NZ) * DEPTH, DEPTH)
                for r in range(2):
                    part = lax.dot_general(xbuf[d, r, :, pl.ds(start, DEPTH)], wbuf[s], (((1,), (1,)), ((), ())),
                                           preferred_element_type=jnp.float32)
                    if first and s == sets[0]:
                        acc[d, r] = part
                    else:
                        acc[d, r] += part

    lane = lax.broadcasted_iota(jnp.int32, (1, COLS), 1)
    column = lane
    for r, (kept, other) in enumerate(((0, 7), (6, 1), (2, 5), (4, 3))):
        block = lax.rem(y + jnp.where(keeper, kept, other), NY)
        column = jnp.where(lane >= r * PART, block * COLS + x * PART + lane - r * PART, column)
    column = column.astype(jnp.float32)
    place = lax.broadcasted_iota(jnp.int32, (ROWS, 128), 1)

    def note_statistics(ds, fresh):
        gathered = jnp.zeros((ROWS, 128), jnp.float32) if fresh else noted[...]
        for d in ds:
            for r in range(2):
                n = 2 * d + r
                logits = acc[d, r]
                largest = jnp.max(logits, axis=1, keepdims=True)
                exp_total = jnp.sum(jnp.exp(logits - largest), axis=1, keepdims=True)
                target = jnp.sum(jnp.where(column == turned[:, n:n + 1], logits, 0.0), axis=1, keepdims=True)
                for which, v in enumerate((largest, exp_total, target)):
                    gathered = jnp.where(place == 8 * which + n, v, gathered)
        noted[...] = gathered

    early = (0, 1, 7, 2, 6)

    def stage_a():
        sib_wait(0)
        multiply((0,), early, True)

    def stage_b():
        sib_wait(1)
        sib_wait(3)
        multiply((1, 3), early, True)

    def stage_c():
        multiply((0, 1, 3), (3, 5))

    def stage_d():
        multiply((0, 1, 3), (4,))

    def stage_e():
        note_statistics((0, 1, 3), True)

    events += [(47, stage_a, ()), (59, stage_b, ()), (64, stage_c, ()), (70, stage_d, ()), (75, stage_e, ())]
    def ev_rest():
        ev_normed(1)
        x_right(1).start()
        ev_normed(2)
        x_left(2).start()
        ev_rows(2)
        ev_rows(3)
        for i in range(NR):
            sib(0, i).start()

    events += [(6.1, ev_near, ()), (40, ev_wanted, ()), (6.2, ev_rest, ())]
    events.sort(key=lambda e: e[0])

    def ev_normed(i):
        raw_copy(i).wait()
        normalise(i)

    ev_normed(0)
    x_right(0).start()
    ev_normed(NR - 1)
    x_left(NR - 1).start()
    ev_targets()
    for _, go, given in events:
        go(*given)
    sib_wait(2)
    multiply((2,), tuple(range(8)), True)
    note_statistics((2,), False)
    turned[...] = noted[...].T
    for d in range(4):
        for r in range(2):
            for which in range(3):
                n = 8 * which + 2 * d + r
                stats[which, pl.ds(owner_of(d, r), 1), :] = turned[n:n + 1, :]

    def st_copy(j):
        return remote(stats, ring_stats.at[j], st_send.at[j], st_recv.at[j], ring(j))

    for j in range(1, 8):
        st_copy(j).start()
    for j in range(1, 8):
        st_copy(j).wait_recv()
    parts = [stats[...]] + [ring_stats[j] for j in range(1, 8)]
    top = parts[0][0]
    for part in parts[1:]:
        top = jnp.maximum(top, part[0])
    total = jnp.zeros((8, 128), jnp.float32)
    picked = jnp.zeros((8, 128), jnp.float32)
    for part in parts:
        total = total + part[1] * jnp.exp(part[0] - top)
        picked = picked + part[2]
    slot_out[...] = picked - (top + jnp.log(total))

    def lp_copy(j):
        return remote(slot_out, slot_in.at[z], lp_send.at[j], lp_recv.at[j], (y, lax.rem(dp + 8 * j, 64)))

    for j in range(1, 8):
        lp_copy(j).start()
    slot_in[z] = slot_out[...]
    for j in range(1, 8):
        source = lax.rem(z + NZ - j, NZ)
        remote(slot_out, slot_in.at[source], lp_send.at[j], lp_recv.at[j], up_z).wait_recv()
    slots = slot_in[...].reshape(64, 128)
    result = jnp.zeros((1, 64), jnp.float32)
    for k in range(2):
        value = jnp.sum(jnp.where(place[:64] == 2 * dp + k, slots, 0.0), axis=1, keepdims=True)
        result = result + jnp.sum(jnp.where(hits[k] > 0.5, value, 0.0), axis=0, keepdims=True)
    out_ref[...] = result

    for step in (1, 2, 3):
        shard_copy(step).wait_send()

    @pl.when(jnp.logical_not(keeper))
    def _():
        shard_copy(0).wait_send()
        for sends in other_sends:
            for send in sends:
                y_copy(*send).wait_send()

    @pl.when(keeper)
    def _():
        for sends in keeper_sends:
            for send in sends:
                y_copy(*send).wait_send()

    for s in range(4):
        for q in range(NK):
            if sends_p(s, q):
                zp(s, q).wait_send()
            if sends_m(s, q):
                zm(s, q).wait_send()
    for i in range(NR):
        x_right(i).wait_send()
        x_left(i).wait_send()
        for d in range(4):
            sib(d, i).wait_send()
    for i in range(NR // 2):
        f_right(i).wait_send()
        f_left_copy(NR - 1 - i).wait_send()
    for j in range(1, 8):
        m_copy(j).wait_send()
        t_copy(j).wait_send()
        st_copy(j).wait_send()
        lp_copy(j).wait_send()


def body(rollout_rows, counts, targets, final_gain, lm_head):
    rows = rollout_rows.reshape(64, 2, FEATURES)
    dma = pltpu.SemaphoreType.DMA
    vmem = pl.BlockSpec(memory_space=pltpu.VMEM)
    hbm = pl.BlockSpec(memory_space=pl.ANY)
    tile = (8, 128)
    f32 = jnp.float32
    log_probs = pl.pallas_call(
        kernel,
        out_shape=jax.ShapeDtypeStruct((1, 64), f32),
        in_specs=[hbm, vmem, vmem, vmem, vmem],
        out_specs=vmem,
        scratch_shapes=[
            pltpu.VMEM((64, 2, FEATURES), jnp.bfloat16),
            pltpu.VMEM((COLS, PIECE), jnp.bfloat16),
            pltpu.VMEM((4, 2, ROWS, FEATURES), jnp.bfloat16),
            pltpu.VMEM((NZ, COLS, DEPTH), jnp.bfloat16),
            pltpu.VMEM((4, 2, ROWS, COLS), f32),
            pltpu.VMEM((NZ, *tile), f32), pltpu.VMEM((NZ, *tile), f32), pltpu.VMEM((8, *tile), f32),
            pltpu.VMEM((2, 64, 64), f32), pltpu.VMEM(tile, f32), pltpu.VMEM((128, 128), f32), pltpu.VMEM((128, 128), f32),
            pltpu.VMEM((3, *tile), f32), pltpu.VMEM((8, 3, *tile), f32),
            pltpu.VMEM(tile, f32), pltpu.VMEM((NZ, *tile), f32),
            dma((NR,)), dma((8,)), dma((8,)), dma((8,)), dma((8,)), dma((8,)), dma((8,)), dma((8,)), dma((8,)),
            dma((NK, 2)), dma((NK,)), dma((4,)), dma((8,)), dma((1,)),
            dma((4, NK)), dma((4, NK)), dma((4, NK)), dma((4, NK)),
            dma((2 * NR,)), dma((2 * NR,)), dma((2 * NR,)), dma((2 * NR,)),
            dma((4, NR)), dma((4, NR)),
        ],
        compiler_params=pltpu.CompilerParams(
            collective_id=0, has_side_effects=True, vmem_limit_bytes=60 * 2**20),
        cost_estimate=pl.CostEstimate(flops=2 * 1024 * COLS * FEATURES, bytes_accessed=8 * 2**20, transcendentals=0),
    )(rows, lm_head, counts[0], targets, final_gain.reshape(1, FEATURES))
    return log_probs.reshape(1, 1, 64)


def solution(mesh):
    in_specs = (
        P("pipe", "dp", None, None, None),
        P("pipe", "dp", None),
        P("dp", None, None),
        P(),
        P("dp", "pipe"),
    )
    out_specs = P("pipe", "dp", None)
    return jax.shard_map(body, mesh=mesh, in_specs=in_specs, out_specs=out_specs, check_vma=False)
```

```python
import jax
import jax.numpy as jnp
from jax import lax
from jax.experimental import pallas as pl
from jax.experimental.pallas import tpu as pltpu
from jax.sharding import PartitionSpec as P

NX, NY, NZ, NC = 4, 8, 8, 2
ROWS = 128
FEATURES = 8192
COLS = 384
DEPTH = FEATURES // NZ
PIECE = 128
NK = 4
PART = COLS // NK
NR = 4
RC = ROWS // NR
MESH = pl.DeviceIdType.MESH


def kernel(x_in, w_hbm, counts_hbm, targets_hbm, gain_hbm, out_ref, w_in, counts_ref, targets_ref, gain_ref, in_sem, raw, flipped, xbuf, wbuf, acc,
           messages, near_targets, ring_targets, hits, wanted, turned, noted, stats, ring_stats, slot_out, slot_in,
           raw_sem, m_send, m_recv, t_send, t_recv, st_send, st_recv, lp_send, lp_recv, y_send, y_recv, p_send, p_recv, p_own,
           zp_send, zp_recv, zm_send, zm_recv, xr_send, xr_recv, xl_send, xl_recv,
           s_send, s_recv):
    y = lax.axis_index("pipe")
    dp = lax.axis_index("dp")
    c = lax.rem(dp, 2)
    x = lax.rem(dp // 2, NX)
    z = dp // (2 * NX)

    def at(zz, xx, cc):
        return (zz * NX + xx) * 2 + cc

    right = (y, at(z, lax.rem(x + 1, NX), c))
    left = (y, at(z, lax.rem(x + NX - 1, NX), c))
    sibling = (y, at(z, x, 1 - c))
    up_z = (y, at(lax.rem(z + 1, NZ), x, c))
    down_z = (y, at(lax.rem(z + NZ - 1, NZ), x, c))
    up_y = (lax.rem(y + 1, NY), dp)
    down_y = (lax.rem(y + NY - 1, NY), dp)
    me8 = lax.rem(dp, 8)
    keeper = lax.rem(y, 2) == c

    def raw_copy(i):
        return pltpu.make_async_copy(x_in.at[pl.ds(i * RC // 2, RC // 2)], raw.at[pl.ds(i * RC // 2, RC // 2)], raw_sem.at[i])

    def rows(ref, i):
        return ref.at[pl.ds(i * RC, RC)]

    fetches = [pltpu.make_async_copy(src, dst, in_sem.at[n]) for n, (src, dst) in enumerate((
        (w_hbm, w_in), (gain_hbm, gain_ref), (counts_hbm, counts_ref), (targets_hbm, targets_ref)))]
    fetches[0].start()
    raw_copy(0).start()
    fetches[1].start()
    for i in range(1, NR):
        raw_copy(i).start()
    fetches[2].start()
    fetches[3].start()

    barrier = pltpu.get_barrier_semaphore()
    for step in range(1, 8):
        pl.semaphore_signal(barrier, inc=1, device_id=(y, z * 8 + lax.rem(me8 + step, 8)), device_id_type=MESH)
        pl.semaphore_signal(barrier, inc=1, device_id=(y, lax.rem(dp + 8 * step, 64)), device_id_type=MESH)
    for other in (up_y, down_y):
        pl.semaphore_signal(barrier, inc=1, device_id=other, device_id_type=MESH)
    fetches[0].wait()
    flipped[...] = w_in[...].astype(jnp.float32).T.astype(jnp.bfloat16)
    pl.semaphore_wait(barrier, 16)

    def remote(src, dst, send, recv, device):
        return pltpu.make_async_remote_copy(
            src_ref=src, dst_ref=dst, send_sem=send, recv_sem=recv, device_id=device, device_id_type=MESH)

    def shard_copy(step):
        other = lax.rem(x + step, NX)
        return remote(flipped.at[pl.ds(pl.multiple_of(other * PART, PART), PART)],
                      wbuf.at[0, pl.ds(0, PART), pl.ds(pl.multiple_of(me8 * PIECE, PIECE), PIECE)],
                      p_send.at[step], p_recv.at[me8], (y, at(z, other, lax.rem(y, 2))))

    def own_shard():
        return pltpu.make_async_copy(
            flipped.at[pl.ds(pl.multiple_of(x * PART, PART), PART)],
            wbuf.at[0, pl.ds(0, PART), pl.ds(pl.multiple_of(me8 * PIECE, PIECE), PIECE)], p_own.at[0])

    for step in (2, 1, 3):
        shard_copy(step).start()

    @pl.when(keeper)
    def _():
        own_shard().start()

    @pl.when(jnp.logical_not(keeper))
    def _():
        shard_copy(0).start()

    def x_right(i):
        return remote(rows(xbuf.at[0, 0], i), rows(xbuf.at[1, 0], i), xr_send.at[i], xr_recv.at[i], right)

    def x_left(i):
        return remote(rows(xbuf.at[0, 0], i), rows(xbuf.at[3, 0], i), xl_send.at[i], xl_recv.at[i], left)

    def f_right(i):
        return remote(rows(xbuf.at[1, 0], i), rows(xbuf.at[2, 0], i), xr_send.at[NR + i], xr_recv.at[NR + i], right)

    def sib(d, i):
        return remote(rows(xbuf.at[d, 0], i), rows(xbuf.at[d, 1], i), s_send.at[d, i], s_recv.at[d, i], sibling)

    def normalise(i):
        for b in range(i * RC, (i + 1) * RC, 16):
            here = pl.ds(b, 16)
            pairs = pl.ds(b // 2, 8)

            def add(j, total):
                lanes = pl.ds(pl.multiple_of(j * 1024, 1024), 1024)
                v = raw[pairs, :, lanes].reshape(16, 1024)
                xbuf[0, 0, here, lanes] = v
                v = v.astype(jnp.float32)
                v = v * v
                for n in range(8):
                    total = total + v[:, n * 128:(n + 1) * 128]
                return total

            total = lax.fori_loop(0, FEATURES // 1024, add, jnp.zeros((16, 128), jnp.float32))
            scaling = lax.rsqrt(jnp.sum(total, axis=-1, keepdims=True) / FEATURES + 1e-06)

            def put(j, carry):
                lanes = pl.ds(pl.multiple_of(j * 1024, 1024), 1024)
                v = xbuf[0, 0, here, lanes].astype(jnp.float32)
                xbuf[0, 0, here, lanes] = (v * scaling * gain_ref[:, lanes]).astype(jnp.bfloat16)
                return carry

            lax.fori_loop(0, FEATURES // 1024, put, 0)

    def m_copy(j):
        return remote(messages.at[lax.rem(z + j, NZ)], near_targets.at[j], m_send.at[j], m_recv.at[j],
                      (y, lax.rem(dp + 8 * j, 64)))

    def ring(j):
        return (y, z * 8 + lax.rem(me8 + j, 8))

    def t_copy(j):
        return remote(ring_targets.at[0], ring_targets.at[j], t_send.at[j], t_recv.at[j], ring(j))

    def ev_targets():
        held = counts_ref[...].astype(jnp.float32)
        mine = targets_ref[0, pl.ds(y, 1), :].astype(jnp.float32)
        lane = lax.broadcasted_iota(jnp.int32, (64, 64), 1)
        row = lax.broadcasted_iota(jnp.int32, (64, 64), 0)
        start = jnp.sum(jnp.where(lane < row, held, 0.0), axis=1, keepdims=True)
        number = jnp.sum(jnp.where(lane == row, held, 0.0), axis=1, keepdims=True)
        place = lax.broadcasted_iota(jnp.int32, (64, 128), 1)
        made = jnp.zeros((64, 128), jnp.float32)
        for k in range(2):
            at_row = jnp.where(number > k, start + k, -1.0)
            hit = lane.astype(jnp.float32) == at_row
            hits[k] = jnp.where(hit, 1.0, 0.0)
            target = jnp.sum(jnp.where(hit, mine, 0.0), axis=1, keepdims=True)
            made = made + jnp.where(place == 2 * dp + k, target, 0.0)
        messages[...] = made.reshape(NZ, 8, 128)
        for j in range(1, 8):
            m_copy(j).start()

    def ev_near():
        total = messages[z]
        for j in range(1, 8):
            m_copy(j).wait_recv()
            total = total + near_targets[j]
        ring_targets[0] = total
        for j in range(1, 8):
            t_copy(j).start()

    def owner_of(d, r):
        return lax.rem(x + (NX - d), NX) * 2 + (c if r == 0 else 1 - c)

    def ev_wanted():
        total = ring_targets[0]
        for j in range(1, 8):
            t_copy(j).wait_recv()
            total = total + ring_targets[j]
        wanted[...] = total
        turned[...] = jnp.zeros((128, 128), jnp.float32)
        for d in range(4):
            for r in range(2):
                turned[2 * d + r:2 * d + r + 1, :] = wanted[pl.ds(owner_of(d, r), 1), :]
        turned[...] = turned[...].T

    def chunk(s, r):
        return wbuf.at[s, pl.ds(r * PART, PART)]

    def y_copy(r, to, way):
        return remote(chunk(0, r), chunk(0, to), y_send.at[r, way], y_recv.at[to], (up_y, down_y)[way])

    keeper_sends = (((0, 0, 0), (0, 1, 1)), ((1, 2, 0),), ((2, 3, 1),), ())
    other_sends = (((0, 1, 0),), ((1, 2, 1),), ((2, 3, 0),), ())

    def zp(s, q):
        return remote(chunk(s, q), chunk(s + 1, q), zp_send.at[s, q], zp_recv.at[s, q], up_z)

    def zm(s, q):
        return remote(chunk((8 - s) % 8, q), chunk(7 - s, q), zm_send.at[s, q], zm_recv.at[s, q], down_z)

    def sends_p(s, q):
        return s < 3 or (s == 3 and q < NK // 2)

    def sends_m(s, q):
        return s < 3 or (s == 3 and q >= NK // 2)

    events = []

    def ev_part(r):
        @pl.when(keeper)
        def _():
            if r == 0:
                own_shard().wait()
                for i in range(1, 8):
                    source = lax.rem(me8 + i, 8)
                    remote(flipped.at[pl.ds(0, PART)], wbuf.at[0, pl.ds(0, PART), pl.ds(0, PIECE)],
                           p_send.at[0], p_recv.at[source], right).wait_recv()
            else:
                y_copy(r, r, 0).wait_recv()
            for send in keeper_sends[r]:
                y_copy(*send).start()

        @pl.when(jnp.logical_not(keeper))
        def _():
            y_copy(r, r, 0).wait_recv()
            for send in other_sends[r]:
                y_copy(*send).start()

        zp(0, r).start()
        zm(0, r).start()

    def ev_zp(s, q):
        zp(s, q).wait_recv()
        if sends_p(s + 1, q):
            zp(s + 1, q).start()

    def ev_zm(s, q):
        zm(s, q).wait_recv()
        if sends_m(s + 1, q):
            zm(s + 1, q).start()

    def ev_rows(n):
        x_right(n).start()
        x_left(NR - 1 - n).start()

    def ev_right(i):
        x_right(i).wait_recv()
        sib(1, i).start()
        if i < NR // 2:
            f_right(i).start()

    def f_left_copy(i):
        return remote(rows(xbuf.at[3, 0], i), rows(xbuf.at[2, 0], i), xl_send.at[NR + i], xl_recv.at[NR + i], left)

    def ev_left(i):
        x_left(i).wait_recv()
        sib(3, i).start()
        if i >= NR // 2:
            f_left_copy(i).start()

    def ev_opp_right(i):
        f_right(i).wait_recv()
        sib(2, i).start()

    def ev_opp_left(i):
        f_left_copy(i).wait_recv()
        sib(2, i).start()

    for r, t in enumerate((6, 13, 15, 22)):
        events.append((t, ev_part, (r,)))
    for s, times in enumerate(((14, 18, 24, 29), (33, 37, 41, 45), (50, 54, 58, 62), (66, 67, 68, 69))):
        for q, t in enumerate(times):
            if sends_p(s, q):
                events.append((t, ev_zp, (s, q)))
            if sends_m(s, q):
                events.append((t, ev_zm, (s, q)))
    for i, t in enumerate((25, 34, 45.5, 58.5)):
        events.append((t, ev_right, (i,)))
        events.append((t, ev_left, (NR - 1 - i,)))
    for i, t in enumerate((65.8, 69.5)):
        events.append((t, ev_opp_right, (i,)))
        events.append((t, ev_opp_left, (NR - 1 - i,)))

    def sib_wait(d):
        for i in range(NR):
            sib(d, i).wait_recv()

    def multiply(ds, sets, first=False):
        for d in ds:
            for s in sets:
                start = pl.multiple_of(lax.rem(z - s + NZ, NZ) * DEPTH, DEPTH)
                both = xbuf[d, :, :, pl.ds(start, DEPTH)].reshape(2 * ROWS, DEPTH)
                part = lax.dot_general(both, wbuf[s], (((1,), (1,)), ((), ())), preferred_element_type=jnp.float32)
                part = part.reshape(2, ROWS, COLS)
                if first and s == sets[0]:
                    acc[d] = part
                else:
                    acc[d] += part

    lane = lax.broadcasted_iota(jnp.int32, (1, COLS), 1)
    column = lane
    for r, (kept, other) in enumerate(((0, 7), (6, 1), (2, 5), (4, 3))):
        block = lax.rem(y + jnp.where(keeper, kept, other), NY)
        column = jnp.where(lane >= r * PART, block * COLS + x * PART + lane - r * PART, column)
    column = column.astype(jnp.float32)
    place = lax.broadcasted_iota(jnp.int32, (ROWS, 128), 1)

    def note_statistics(ds, fresh):
        gathered = jnp.zeros((ROWS, 128), jnp.float32) if fresh else noted[...]
        for d in ds:
            for r in range(2):
                n = 2 * d + r
                logits = acc[d, r]
                largest = jnp.max(logits, axis=1, keepdims=True)
                exp_total = jnp.sum(jnp.exp(logits - largest), axis=1, keepdims=True)
                target = jnp.sum(jnp.where(column == turned[:, n:n + 1], logits, 0.0), axis=1, keepdims=True)
                for which, v in enumerate((largest, exp_total, target)):
                    gathered = jnp.where(place == 8 * which + n, v, gathered)
        noted[...] = gathered

    early = (0, 1, 7, 2, 6)

    def stage_a():
        sib_wait(0)
        multiply((0,), early, True)

    def stage_b():
        sib_wait(1)
        sib_wait(3)
        multiply((1, 3), early, True)

    def stage_c():
        multiply((0, 1, 3), (3, 5))

    def stage_d():
        multiply((0, 1, 3), (4,))

    def stage_e():
        note_statistics((0, 1, 3), True)

    events += [(47, stage_a, ()), (62.5, stage_b, ()), (64, stage_c, ()), (70, stage_d, ()), (75, stage_e, ())]
    def ev_rest():
        ev_normed(1)
        x_right(1).start()
        ev_normed(2)
        x_left(2).start()
        ev_rows(2)
        ev_rows(3)
        for i in range(NR):
            sib(0, i).start()

    events += [(6.1, ev_near, ()), (40, ev_wanted, ()), (6.2, ev_rest, ())]
    events.sort(key=lambda e: e[0])

    def ev_normed(i):
        raw_copy(i).wait()
        normalise(i)

    fetches[1].wait()
    ev_normed(0)
    x_right(0).start()
    ev_normed(NR - 1)
    x_left(NR - 1).start()
    fetches[2].wait()
    fetches[3].wait()
    ev_targets()
    for _, go, given in events:
        go(*given)
    sib_wait(2)
    multiply((2,), tuple(range(8)), True)
    note_statistics((2,), False)
    turned[...] = noted[...].T
    for d in range(4):
        for r in range(2):
            for which in range(3):
                n = 8 * which + 2 * d + r
                stats[which, pl.ds(owner_of(d, r), 1), :] = turned[n:n + 1, :]

    def st_copy(j):
        return remote(stats, ring_stats.at[j], st_send.at[j], st_recv.at[j], ring(j))

    for j in (4, 3, 5, 2, 6, 1, 7):
        st_copy(j).start()
    for j in range(1, 8):
        st_copy(j).wait_recv()
    parts = [stats[...]] + [ring_stats[j] for j in range(1, 8)]
    top = parts[0][0]
    for part in parts[1:]:
        top = jnp.maximum(top, part[0])
    total = jnp.zeros((8, 128), jnp.float32)
    picked = jnp.zeros((8, 128), jnp.float32)
    for part in parts:
        total = total + part[1] * jnp.exp(part[0] - top)
        picked = picked + part[2]
    slot_out[...] = picked - (top + jnp.log(total))

    def lp_copy(j):
        return remote(slot_out, slot_in.at[z], lp_send.at[j], lp_recv.at[j], (y, lax.rem(dp + 8 * j, 64)))

    for j in (4, 3, 5, 2, 6, 1, 7):
        lp_copy(j).start()
    slot_in[z] = slot_out[...]
    for j in range(1, 8):
        source = lax.rem(z + NZ - j, NZ)
        remote(slot_out, slot_in.at[source], lp_send.at[j], lp_recv.at[j], up_z).wait_recv()
    slots = slot_in[...].reshape(64, 128)
    result = jnp.zeros((1, 64), jnp.float32)
    for k in range(2):
        value = jnp.sum(jnp.where(place[:64] == 2 * dp + k, slots, 0.0), axis=1, keepdims=True)
        result = result + jnp.sum(jnp.where(hits[k] > 0.5, value, 0.0), axis=0, keepdims=True)
    out_ref[...] = result

    for step in (1, 2, 3):
        shard_copy(step).wait_send()

    @pl.when(jnp.logical_not(keeper))
    def _():
        shard_copy(0).wait_send()
        for sends in other_sends:
            for send in sends:
                y_copy(*send).wait_send()

    @pl.when(keeper)
    def _():
        for sends in keeper_sends:
            for send in sends:
                y_copy(*send).wait_send()

    for s in range(4):
        for q in range(NK):
            if sends_p(s, q):
                zp(s, q).wait_send()
            if sends_m(s, q):
                zm(s, q).wait_send()
    for i in range(NR):
        x_right(i).wait_send()
        x_left(i).wait_send()
        for d in range(4):
            sib(d, i).wait_send()
    for i in range(NR // 2):
        f_right(i).wait_send()
        f_left_copy(NR - 1 - i).wait_send()
    for j in range(1, 8):
        m_copy(j).wait_send()
        t_copy(j).wait_send()
        st_copy(j).wait_send()
        lp_copy(j).wait_send()


def body(rollout_rows, counts, targets, final_gain, lm_head):
    rows = rollout_rows.reshape(64, 2, FEATURES)
    dma = pltpu.SemaphoreType.DMA
    vmem = pl.BlockSpec(memory_space=pltpu.VMEM)
    hbm = pl.BlockSpec(memory_space=pl.ANY)
    tile = (8, 128)
    f32 = jnp.float32
    log_probs = pl.pallas_call(
        kernel,
        out_shape=jax.ShapeDtypeStruct((1, 64), f32),
        in_specs=[hbm] * 5,
        out_specs=vmem,
        scratch_shapes=[
            pltpu.VMEM((PIECE, COLS), jnp.bfloat16), pltpu.VMEM((1, 64), jnp.int32), pltpu.VMEM((1, NY, 64), jnp.int32),
            pltpu.VMEM((1, FEATURES), f32), dma((4,)),
            pltpu.VMEM((64, 2, FEATURES), jnp.bfloat16),
            pltpu.VMEM((COLS, PIECE), jnp.bfloat16),
            pltpu.VMEM((4, 2, ROWS, FEATURES), jnp.bfloat16),
            pltpu.VMEM((NZ, COLS, DEPTH), jnp.bfloat16),
            pltpu.VMEM((4, 2, ROWS, COLS), f32),
            pltpu.VMEM((NZ, *tile), f32), pltpu.VMEM((NZ, *tile), f32), pltpu.VMEM((8, *tile), f32),
            pltpu.VMEM((2, 64, 64), f32), pltpu.VMEM(tile, f32), pltpu.VMEM((128, 128), f32), pltpu.VMEM((128, 128), f32),
            pltpu.VMEM((3, *tile), f32), pltpu.VMEM((8, 3, *tile), f32),
            pltpu.VMEM(tile, f32), pltpu.VMEM((NZ, *tile), f32),
            dma((NR,)), dma((8,)), dma((8,)), dma((8,)), dma((8,)), dma((8,)), dma((8,)), dma((8,)), dma((8,)),
            dma((NK, 2)), dma((NK,)), dma((4,)), dma((8,)), dma((1,)),
            dma((4, NK)), dma((4, NK)), dma((4, NK)), dma((4, NK)),
            dma((2 * NR,)), dma((2 * NR,)), dma((2 * NR,)), dma((2 * NR,)),
            dma((4, NR)), dma((4, NR)),
        ],
        compiler_params=pltpu.CompilerParams(
            collective_id=0, has_side_effects=True, vmem_limit_bytes=60 * 2**20),
        cost_estimate=pl.CostEstimate(flops=2 * 1024 * COLS * FEATURES, bytes_accessed=8 * 2**20, transcendentals=0),
    )(rows, lm_head, counts[0], targets, final_gain.reshape(1, FEATURES))
    return log_probs.reshape(1, 1, 64)


def solution(mesh):
    in_specs = (
        P("pipe", "dp", None, None, None),
        P("pipe", "dp", None),
        P("dp", None, None),
        P(),
        P("dp", "pipe"),
    )
    out_specs = P("pipe", "dp", None)
    return jax.shard_map(body, mesh=mesh, in_specs=in_specs, out_specs=out_specs, check_vma=False)
```

```python
import jax
import jax.numpy as jnp
from jax import lax
from jax.experimental import pallas as pl
from jax.experimental.pallas import tpu as pltpu
from jax.sharding import PartitionSpec as P

NX, NY, NZ, NC = 4, 8, 8, 2
ROWS = 128
FEATURES = 8192
COLS = 384
DEPTH = FEATURES // NZ
PIECE = 128
NK = 4
PART = COLS // NK
NR = 4
RC = ROWS // NR
MESH = pl.DeviceIdType.MESH


def kernel(x_in, w_hbm, counts_hbm, targets_hbm, gain_hbm, out_ref, w_in, counts_ref, targets_ref, gain_ref, in_sem, raw, flipped, xbuf, wbuf, acc,
           messages, near_targets, ring_targets, hits, wanted, turned, noted, stats, ring_stats, slot_out, slot_in,
           raw_sem, m_send, m_recv, t_send, t_recv, st_send, st_recv, lp_send, lp_recv, y_send, y_recv, p_send, p_recv, p_own,
           zp_send, zp_recv, zm_send, zm_recv, xr_send, xr_recv, xl_send, xl_recv,
           s_send, s_recv):
    y = lax.axis_index("pipe")
    dp = lax.axis_index("dp")
    c = lax.rem(dp, 2)
    x = lax.rem(dp // 2, NX)
    z = dp // (2 * NX)

    def at(zz, xx, cc):
        return (zz * NX + xx) * 2 + cc

    right = (y, at(z, lax.rem(x + 1, NX), c))
    left = (y, at(z, lax.rem(x + NX - 1, NX), c))
    sibling = (y, at(z, x, 1 - c))
    up_z = (y, at(lax.rem(z + 1, NZ), x, c))
    down_z = (y, at(lax.rem(z + NZ - 1, NZ), x, c))
    up_y = (lax.rem(y + 1, NY), dp)
    down_y = (lax.rem(y + NY - 1, NY), dp)
    me8 = lax.rem(dp, 8)
    keeper = lax.rem(y, 2) == c

    def raw_copy(i):
        return pltpu.make_async_copy(x_in.at[pl.ds(i * RC // 2, RC // 2)], raw.at[pl.ds(i * RC // 2, RC // 2)], raw_sem.at[i])

    def rows(ref, i):
        return ref.at[pl.ds(i * RC, RC)]

    fetches = [pltpu.make_async_copy(src, dst, in_sem.at[n]) for n, (src, dst) in enumerate((
        (w_hbm, w_in), (gain_hbm, gain_ref), (counts_hbm, counts_ref), (targets_hbm, targets_ref)))]
    fetches[0].start()
    raw_copy(0).start()
    fetches[1].start()
    for i in range(1, NR):
        raw_copy(i).start()
    fetches[2].start()
    fetches[3].start()

    barrier = pltpu.get_barrier_semaphore()
    for step in range(1, 8):
        pl.semaphore_signal(barrier, inc=1, device_id=(y, z * 8 + lax.rem(me8 + step, 8)), device_id_type=MESH)
        pl.semaphore_signal(barrier, inc=1, device_id=(y, lax.rem(dp + 8 * step, 64)), device_id_type=MESH)
    for other in (up_y, down_y):
        pl.semaphore_signal(barrier, inc=1, device_id=other, device_id_type=MESH)
    fetches[0].wait()
    flipped[...] = w_in[...].astype(jnp.float32).T.astype(jnp.bfloat16)
    def normalise(i):
        for b in range(i * RC, (i + 1) * RC, 16):
            here = pl.ds(b, 16)
            pairs = pl.ds(b // 2, 8)

            def add(j, total):
                lanes = pl.ds(pl.multiple_of(j * 1024, 1024), 1024)
                v = raw[pairs, :, lanes].reshape(16, 1024)
                xbuf[0, 0, here, lanes] = v
                v = v.astype(jnp.float32)
                v = v * v
                for n in range(8):
                    total = total + v[:, n * 128:(n + 1) * 128]
                return total

            total = lax.fori_loop(0, FEATURES // 1024, add, jnp.zeros((16, 128), jnp.float32))
            scaling = lax.rsqrt(jnp.sum(total, axis=-1, keepdims=True) / FEATURES + 1e-06)

            def put(j, carry):
                lanes = pl.ds(pl.multiple_of(j * 1024, 1024), 1024)
                v = xbuf[0, 0, here, lanes].astype(jnp.float32)
                xbuf[0, 0, here, lanes] = (v * scaling * gain_ref[:, lanes]).astype(jnp.bfloat16)
                return carry

            lax.fori_loop(0, FEATURES // 1024, put, 0)

    def ev_normed(i):
        raw_copy(i).wait()
        normalise(i)

    fetches[1].wait()
    ev_normed(0)
    ev_normed(NR - 1)
    pl.semaphore_wait(barrier, 16)

    def remote(src, dst, send, recv, device):
        return pltpu.make_async_remote_copy(
            src_ref=src, dst_ref=dst, send_sem=send, recv_sem=recv, device_id=device, device_id_type=MESH)

    def shard_copy(step):
        other = lax.rem(x + step, NX)
        return remote(flipped.at[pl.ds(pl.multiple_of(other * PART, PART), PART)],
                      wbuf.at[0, pl.ds(0, PART), pl.ds(pl.multiple_of(me8 * PIECE, PIECE), PIECE)],
                      p_send.at[step], p_recv.at[me8], (y, at(z, other, lax.rem(y, 2))))

    def own_shard():
        return pltpu.make_async_copy(
            flipped.at[pl.ds(pl.multiple_of(x * PART, PART), PART)],
            wbuf.at[0, pl.ds(0, PART), pl.ds(pl.multiple_of(me8 * PIECE, PIECE), PIECE)], p_own.at[0])

    for step in (2, 1, 3):
        shard_copy(step).start()

    @pl.when(keeper)
    def _():
        own_shard().start()

    @pl.when(jnp.logical_not(keeper))
    def _():
        shard_copy(0).start()

    def x_right(i):
        return remote(rows(xbuf.at[0, 0], i), rows(xbuf.at[1, 0], i), xr_send.at[i], xr_recv.at[i], right)

    def x_left(i):
        return remote(rows(xbuf.at[0, 0], i), rows(xbuf.at[3, 0], i), xl_send.at[i], xl_recv.at[i], left)

    def f_right(i):
        return remote(rows(xbuf.at[1, 0], i), rows(xbuf.at[2, 0], i), xr_send.at[NR + i], xr_recv.at[NR + i], right)

    def sib(d, i):
        return remote(rows(xbuf.at[d, 0], i), rows(xbuf.at[d, 1], i), s_send.at[d, i], s_recv.at[d, i], sibling)

    x_right(0).start()
    x_left(NR - 1).start()

    def m_copy(j):
        return remote(messages.at[lax.rem(z + j, NZ)], near_targets.at[j], m_send.at[j], m_recv.at[j],
                      (y, lax.rem(dp + 8 * j, 64)))

    def ring(j):
        return (y, z * 8 + lax.rem(me8 + j, 8))

    def t_copy(j):
        return remote(ring_targets.at[0], ring_targets.at[j], t_send.at[j], t_recv.at[j], ring(j))

    def ev_targets():
        held = counts_ref[...].astype(jnp.float32)
        mine = targets_ref[0, pl.ds(y, 1), :].astype(jnp.float32)
        lane = lax.broadcasted_iota(jnp.int32, (64, 64), 1)
        row = lax.broadcasted_iota(jnp.int32, (64, 64), 0)
        start = jnp.sum(jnp.where(lane < row, held, 0.0), axis=1, keepdims=True)
        number = jnp.sum(jnp.where(lane == row, held, 0.0), axis=1, keepdims=True)
        place = lax.broadcasted_iota(jnp.int32, (64, 128), 1)
        made = jnp.zeros((64, 128), jnp.float32)
        for k in range(2):
            at_row = jnp.where(number > k, start + k, -1.0)
            hit = lane.astype(jnp.float32) == at_row
            hits[k] = jnp.where(hit, 1.0, 0.0)
            target = jnp.sum(jnp.where(hit, mine, 0.0), axis=1, keepdims=True)
            made = made + jnp.where(place == 2 * dp + k, target, 0.0)
        messages[...] = made.reshape(NZ, 8, 128)
        for j in range(1, 8):
            m_copy(j).start()

    def ev_near():
        total = messages[z]
        for j in range(1, 8):
            m_copy(j).wait_recv()
            total = total + near_targets[j]
        ring_targets[0] = total
        for j in range(1, 8):
            t_copy(j).start()

    def owner_of(d, r):
        return lax.rem(x + (NX - d), NX) * 2 + (c if r == 0 else 1 - c)

    def ev_wanted():
        total = ring_targets[0]
        for j in range(1, 8):
            t_copy(j).wait_recv()
            total = total + ring_targets[j]
        wanted[...] = total
        turned[...] = jnp.zeros((128, 128), jnp.float32)
        for d in range(4):
            for r in range(2):
                turned[2 * d + r:2 * d + r + 1, :] = wanted[pl.ds(owner_of(d, r), 1), :]
        turned[...] = turned[...].T

    def chunk(s, r):
        return wbuf.at[s, pl.ds(r * PART, PART)]

    def y_copy(r, to, way):
        return remote(chunk(0, r), chunk(0, to), y_send.at[r, way], y_recv.at[to], (up_y, down_y)[way])

    keeper_sends = (((0, 0, 0), (0, 1, 1)), ((1, 2, 0),), ((2, 3, 1),), ())
    other_sends = (((0, 1, 0),), ((1, 2, 1),), ((2, 3, 0),), ())

    def zp(s, q):
        return remote(chunk(s, q), chunk(s + 1, q), zp_send.at[s, q], zp_recv.at[s, q], up_z)

    def zm(s, q):
        return remote(chunk((8 - s) % 8, q), chunk(7 - s, q), zm_send.at[s, q], zm_recv.at[s, q], down_z)

    def sends_p(s, q):
        return s < 3 or (s == 3 and q < NK // 2)

    def sends_m(s, q):
        return s < 3 or (s == 3 and q >= NK // 2)

    events = []

    def ev_part(r):
        @pl.when(keeper)
        def _():
            if r == 0:
                own_shard().wait()
                for i in range(1, 8):
                    source = lax.rem(me8 + i, 8)
                    remote(flipped.at[pl.ds(0, PART)], wbuf.at[0, pl.ds(0, PART), pl.ds(0, PIECE)],
                           p_send.at[0], p_recv.at[source], right).wait_recv()
            else:
                y_copy(r, r, 0).wait_recv()
            for send in keeper_sends[r]:
                y_copy(*send).start()

        @pl.when(jnp.logical_not(keeper))
        def _():
            y_copy(r, r, 0).wait_recv()
            for send in other_sends[r]:
                y_copy(*send).start()

        zp(0, r).start()
        zm(0, r).start()

    def ev_zp(s, q):
        zp(s, q).wait_recv()
        if sends_p(s + 1, q):
            zp(s + 1, q).start()

    def ev_zm(s, q):
        zm(s, q).wait_recv()
        if sends_m(s + 1, q):
            zm(s + 1, q).start()

    def ev_rows(n):
        x_right(n).start()
        x_left(NR - 1 - n).start()

    def ev_right(i):
        x_right(i).wait_recv()
        sib(1, i).start()
        if i < NR // 2:
            f_right(i).start()

    def f_left_copy(i):
        return remote(rows(xbuf.at[3, 0], i), rows(xbuf.at[2, 0], i), xl_send.at[NR + i], xl_recv.at[NR + i], left)

    def ev_left(i):
        x_left(i).wait_recv()
        sib(3, i).start()
        if i >= NR // 2:
            f_left_copy(i).start()

    def ev_opp_right(i):
        f_right(i).wait_recv()
        sib(2, i).start()

    def ev_opp_left(i):
        f_left_copy(i).wait_recv()
        sib(2, i).start()

    for r, t in enumerate((6, 13, 15, 22)):
        events.append((t, ev_part, (r,)))
    for s, times in enumerate(((14, 18, 24, 29), (33, 37, 41, 45), (50, 54, 58, 62), (66, 67, 68, 69))):
        for q, t in enumerate(times):
            if sends_p(s, q):
                events.append((t, ev_zp, (s, q)))
            if sends_m(s, q):
                events.append((t, ev_zm, (s, q)))
    for i, t in enumerate((25, 34, 45.5, 58.5)):
        events.append((t, ev_right, (i,)))
        events.append((t, ev_left, (NR - 1 - i,)))
    for i, t in enumerate((65.8, 69.5)):
        events.append((t, ev_opp_right, (i,)))
        events.append((t, ev_opp_left, (NR - 1 - i,)))

    def sib_wait(d):
        for i in range(NR):
            sib(d, i).wait_recv()

    def multiply(ds, sets, first=False):
        for d in ds:
            for s in sets:
                start = pl.multiple_of(lax.rem(z - s + NZ, NZ) * DEPTH, DEPTH)
                both = xbuf[d, :, :, pl.ds(start, DEPTH)].reshape(2 * ROWS, DEPTH)
                part = lax.dot_general(both, wbuf[s], (((1,), (1,)), ((), ())), preferred_element_type=jnp.float32)
                part = part.reshape(2, ROWS, COLS)
                if first and s == sets[0]:
                    acc[d] = part
                else:
                    acc[d] += part

    lane = lax.broadcasted_iota(jnp.int32, (1, COLS), 1)
    column = lane
    for r, (kept, other) in enumerate(((0, 7), (6, 1), (2, 5), (4, 3))):
        block = lax.rem(y + jnp.where(keeper, kept, other), NY)
        column = jnp.where(lane >= r * PART, block * COLS + x * PART + lane - r * PART, column)
    column = column.astype(jnp.float32)
    place = lax.broadcasted_iota(jnp.int32, (ROWS, 128), 1)

    def note_statistics(ds, fresh):
        gathered = jnp.zeros((ROWS, 128), jnp.float32) if fresh else noted[...]
        for d in ds:
            for r in range(2):
                n = 2 * d + r
                logits = acc[d, r]
                largest = jnp.max(logits, axis=1, keepdims=True)
                exp_total = jnp.sum(jnp.exp(logits - largest), axis=1, keepdims=True)
                target = jnp.sum(jnp.where(column == turned[:, n:n + 1], logits, 0.0), axis=1, keepdims=True)
                for which, v in enumerate((largest, exp_total, target)):
                    gathered = jnp.where(place == 8 * which + n, v, gathered)
        noted[...] = gathered

    early = (0, 1, 7, 2, 6)

    def stage_a():
        sib_wait(0)
        multiply((0,), early, True)

    def stage_b():
        sib_wait(1)
        sib_wait(3)
        multiply((1, 3), early, True)

    def stage_c():
        multiply((0, 1, 3), (3, 5))

    def stage_d():
        multiply((0, 1, 3), (4,))

    def stage_e():
        note_statistics((0, 1, 3), True)

    events += [(47, stage_a, ()), (62.5, stage_b, ()), (64, stage_c, ()), (70, stage_d, ()), (75, stage_e, ())]
    def ev_rest():
        ev_normed(1)
        x_right(1).start()
        ev_normed(2)
        x_left(2).start()
        ev_rows(2)
        ev_rows(3)
        for i in range(NR):
            sib(0, i).start()

    events += [(6.1, ev_near, ()), (40, ev_wanted, ()), (6.2, ev_rest, ())]
    events.sort(key=lambda e: e[0])

    fetches[2].wait()
    fetches[3].wait()
    ev_targets()
    for _, go, given in events:
        go(*given)
    sib_wait(2)
    multiply((2,), tuple(range(8)), True)
    note_statistics((2,), False)
    turned[...] = noted[...].T
    for d in range(4):
        for r in range(2):
            for which in range(3):
                n = 8 * which + 2 * d + r
                stats[which, pl.ds(owner_of(d, r), 1), :] = turned[n:n + 1, :]

    def st_copy(j):
        return remote(stats, ring_stats.at[j], st_send.at[j], st_recv.at[j], ring(j))

    for j in (4, 3, 5, 2, 6, 1, 7):
        st_copy(j).start()
    for j in range(1, 8):
        st_copy(j).wait_recv()
    parts = [stats[...]] + [ring_stats[j] for j in range(1, 8)]
    top = parts[0][0]
    for part in parts[1:]:
        top = jnp.maximum(top, part[0])
    total = jnp.zeros((8, 128), jnp.float32)
    picked = jnp.zeros((8, 128), jnp.float32)
    for part in parts:
        total = total + part[1] * jnp.exp(part[0] - top)
        picked = picked + part[2]
    slot_out[...] = picked - (top + jnp.log(total))

    def lp_copy(j):
        return remote(slot_out, slot_in.at[z], lp_send.at[j], lp_recv.at[j], (y, lax.rem(dp + 8 * j, 64)))

    for j in (4, 3, 5, 2, 6, 1, 7):
        lp_copy(j).start()
    slot_in[z] = slot_out[...]
    for j in range(1, 8):
        source = lax.rem(z + NZ - j, NZ)
        remote(slot_out, slot_in.at[source], lp_send.at[j], lp_recv.at[j], up_z).wait_recv()
    slots = slot_in[...].reshape(64, 128)
    result = jnp.zeros((1, 64), jnp.float32)
    for k in range(2):
        value = jnp.sum(jnp.where(place[:64] == 2 * dp + k, slots, 0.0), axis=1, keepdims=True)
        result = result + jnp.sum(jnp.where(hits[k] > 0.5, value, 0.0), axis=0, keepdims=True)
    out_ref[...] = result

    for step in (1, 2, 3):
        shard_copy(step).wait_send()

    @pl.when(jnp.logical_not(keeper))
    def _():
        shard_copy(0).wait_send()
        for sends in other_sends:
            for send in sends:
                y_copy(*send).wait_send()

    @pl.when(keeper)
    def _():
        for sends in keeper_sends:
            for send in sends:
                y_copy(*send).wait_send()

    for s in range(4):
        for q in range(NK):
            if sends_p(s, q):
                zp(s, q).wait_send()
            if sends_m(s, q):
                zm(s, q).wait_send()
    for i in range(NR):
        x_right(i).wait_send()
        x_left(i).wait_send()
        for d in range(4):
            sib(d, i).wait_send()
    for i in range(NR // 2):
        f_right(i).wait_send()
        f_left_copy(NR - 1 - i).wait_send()
    for j in range(1, 8):
        m_copy(j).wait_send()
        t_copy(j).wait_send()
        st_copy(j).wait_send()
        lp_copy(j).wait_send()


def body(rollout_rows, counts, targets, final_gain, lm_head):
    rows = rollout_rows.reshape(64, 2, FEATURES)
    dma = pltpu.SemaphoreType.DMA
    vmem = pl.BlockSpec(memory_space=pltpu.VMEM)
    hbm = pl.BlockSpec(memory_space=pl.ANY)
    tile = (8, 128)
    f32 = jnp.float32
    log_probs = pl.pallas_call(
        kernel,
        out_shape=jax.ShapeDtypeStruct((1, 64), f32),
        in_specs=[hbm] * 5,
        out_specs=vmem,
        scratch_shapes=[
            pltpu.VMEM((PIECE, COLS), jnp.bfloat16), pltpu.VMEM((1, 64), jnp.int32), pltpu.VMEM((1, NY, 64), jnp.int32),
            pltpu.VMEM((1, FEATURES), f32), dma((4,)),
            pltpu.VMEM((64, 2, FEATURES), jnp.bfloat16),
            pltpu.VMEM((COLS, PIECE), jnp.bfloat16),
            pltpu.VMEM((4, 2, ROWS, FEATURES), jnp.bfloat16),
            pltpu.VMEM((NZ, COLS, DEPTH), jnp.bfloat16),
            pltpu.VMEM((4, 2, ROWS, COLS), f32),
            pltpu.VMEM((NZ, *tile), f32), pltpu.VMEM((NZ, *tile), f32), pltpu.VMEM((8, *tile), f32),
            pltpu.VMEM((2, 64, 64), f32), pltpu.VMEM(tile, f32), pltpu.VMEM((128, 128), f32), pltpu.VMEM((128, 128), f32),
            pltpu.VMEM((3, *tile), f32), pltpu.VMEM((8, 3, *tile), f32),
            pltpu.VMEM(tile, f32), pltpu.VMEM((NZ, *tile), f32),
            dma((NR,)), dma((8,)), dma((8,)), dma((8,)), dma((8,)), dma((8,)), dma((8,)), dma((8,)), dma((8,)),
            dma((NK, 2)), dma((NK,)), dma((4,)), dma((8,)), dma((1,)),
            dma((4, NK)), dma((4, NK)), dma((4, NK)), dma((4, NK)),
            dma((2 * NR,)), dma((2 * NR,)), dma((2 * NR,)), dma((2 * NR,)),
            dma((4, NR)), dma((4, NR)),
        ],
        compiler_params=pltpu.CompilerParams(
            collective_id=0, has_side_effects=True, vmem_limit_bytes=60 * 2**20),
        cost_estimate=pl.CostEstimate(flops=2 * 1024 * COLS * FEATURES, bytes_accessed=8 * 2**20, transcendentals=0),
    )(rows, lm_head, counts[0], targets, final_gain.reshape(1, FEATURES))
    return log_probs.reshape(1, 1, 64)


def solution(mesh):
    in_specs = (
        P("pipe", "dp", None, None, None),
        P("pipe", "dp", None),
        P("dp", None, None),
        P(),
        P("dp", "pipe"),
    )
    out_specs = P("pipe", "dp", None)
    return jax.shard_map(body, mesh=mesh, in_specs=in_specs, out_specs=out_specs, check_vma=False)
```
